256 devices in a mesh: section: 8 (over z), tensor: 4 (over y), dp: 8 (over x, core).
Axes of the slice: x: 4, y: 4, z: 8, core: 2. Of those that a mesh axis runs over, the one named last changes fastest.
Arguments:
- hidden: bfloat16 [896, 5376], P('dp', ('section', 'tensor')), may hold values from -6 to 6
- head_weight: bfloat16 [5376, 131072], P(None, ('section', 'tensor', 'dp')), may hold values from -0.24549513 to 0.24549513
- targets: int32 [896], replicated, may hold values from 0 to 131071
- response_mask: int32 [896], replicated, may hold values from 0 to 1, as said below
- pair_ids: int32 [16], replicated, may hold values from 0 to 7, as said below
- ref_logprobs: float32 [16], replicated, may hold values from -3 to 3
Outputs:
- logprobs: float32 [16], replicated
- grad_hidden: bfloat16 [896, 5376], P('dp', ('section', 'tensor'))
- grad_weight: bfloat16 [5376, 131072], P(None, ('section', 'tensor', 'dp'))
The draws below stay inside these ranges and needn't reach their ends.
Inputs may be any that keep to these rules, and one draw needn't show every extreme that they name: `pair_ids`: each pair id 0 to 7 names exactly two sequences. `response_mask`: in each sequence the ones form a suffix of at least 28 positions.
All inputs are finite; a program needn't handle non-finite values.
Results may differ from the reference program's by a relative error of at most 0.0046.
Values may be sent and summed in bfloat16 or wider, within the bound.
A program may use at most 128 MiB of HBM per device.

```python
import math
import jax
import jax.numpy as jnp
from jax import lax

D = 5376
SEQ = 56
SEQS = 16
TOKENS = 896
VOCAB = 131072


def draw_head_weight(key, part):
    key = jax.random.fold_in(key, 3)
    step_size = 3.0 / math.sqrt(D)
    values = jax.random.normal(key, (D, VOCAB), jnp.float32)
    return (step_size * jnp.clip(values, -6.0, 6.0)).astype(jnp.bfloat16)


def draw_hidden(key, part):
    key = jax.random.fold_in(key, 4)
    values = jax.random.normal(key, (TOKENS, D), jnp.float32)
    return jnp.clip(values, -6.0, 6.0).astype(jnp.bfloat16)


def draw_response_mask(key, part):
    key = jax.random.fold_in(key, 6)
    prompt_length = jax.random.randint(key, (SEQS,), SEQ // 8, SEQ // 2 + 1)
    position = jnp.arange(TOKENS, dtype=jnp.int32)
    return (position % SEQ >= prompt_length[position // SEQ]).astype(jnp.int32)


def draw_pair_ids(key, part):
    key = jax.random.fold_in(key, 5)
    return (jax.random.permutation(key, SEQS) // 2).astype(jnp.int32)


def touch_ends(drawn, rng, low, high):
    longest = drawn.shape.index(max(drawn.shape))
    spots = []
    for shift in (0, 1):
        where = [jax.random.randint(jax.random.fold_in(rng, axis), (), 0, length) for axis, length in enumerate(drawn.shape)]
        where[longest] = (where[longest] + shift) % drawn.shape[longest]
        spots.append(tuple(where))
    return drawn.at[spots[0]].set(low).at[spots[1]].set(high)


def gaussian(own_key, extent, spread, limit, kind=jnp.bfloat16):
    entries = spread * jax.random.normal(own_key, extent, jnp.float32)
    return jnp.clip(entries, min=-limit, max=limit).astype(kind)


def setup_inputs(seed: int = 0) -> dict:
    streams_of = jax.random.split(jax.random.key(seed), 7)
    return {
        "hidden": draw_hidden(jax.random.fold_in(streams_of[6], 71), 0),
        "head_weight": draw_head_weight(jax.random.fold_in(streams_of[6], 71), 0),
        "targets": touch_ends(jax.random.randint(streams_of[2], (TOKENS,), 0, VOCAB), jax.random.fold_in(streams_of[2], 1), 0, VOCAB - 1).astype(jnp.int32),
        "response_mask": draw_response_mask(jax.random.fold_in(streams_of[6], 71), 0),
        "pair_ids": draw_pair_ids(jax.random.fold_in(streams_of[6], 71), 0),
        "ref_logprobs": gaussian(streams_of[5], (SEQS,), 0.5, 3.0, jnp.float32),
    }


loss_scale = 2048.0
beta_value = 2.0


def pair_coefficients(logprobs, ref_logprobs, pair_ids):
    same = pair_ids[:, None] == pair_ids[None, :]
    order = jnp.arange(pair_ids.shape[0], dtype=jnp.int32)
    earlier = jnp.sum((same & (order[None, :] < order[:, None])).astype(jnp.int32), axis=1)
    signs = jnp.where(earlier == 0, 1.0, -1.0).astype(jnp.float32)
    contrib = signs * (logprobs - ref_logprobs)
    margin = jnp.sum(jnp.where(same, contrib[None, :], 0.0), axis=1)
    return -loss_scale * beta_value * jax.nn.sigmoid(-beta_value * margin) * signs


def reference(hidden, head_weight, targets, response_mask, pair_ids, ref_logprobs):
    logits = jnp.dot(hidden, head_weight, preferred_element_type=jnp.float32)
    row_top = jnp.max(logits, axis=1)
    row_total = jnp.sum(jnp.exp(logits - row_top[:, None]), axis=1)
    log_total = row_top + jnp.log(row_total)
    columns = jnp.arange(VOCAB, dtype=jnp.int32)
    is_target = targets[:, None] == columns[None, :]
    picked = jnp.sum(jnp.where(is_target, logits, 0.0), axis=1)
    mask_float = response_mask.astype(jnp.float32)
    counts = jnp.sum(mask_float.reshape(SEQS, SEQ), axis=1)
    token_terms = (picked - log_total) * mask_float
    logprobs = jnp.sum(token_terms.reshape(SEQS, SEQ), axis=1) / counts
    coefficient = pair_coefficients(logprobs, ref_logprobs, pair_ids)
    token_weight = jnp.repeat(coefficient / counts, SEQ) * mask_float
    probs = jnp.exp(logits - log_total[:, None])
    dlogits = (token_weight[:, None] * (is_target.astype(jnp.float32) - probs)).astype(jnp.bfloat16)
    grad_weight = lax.dot_general(hidden, dlogits, (((0,), (0,)), ((), ())), preferred_element_type=jnp.float32).astype(jnp.bfloat16)
    grad_hidden = lax.dot_general(dlogits, head_weight, (((1,), (1,)), ((), ())), preferred_element_type=jnp.float32).astype(jnp.bfloat16)
    return (logprobs, grad_hidden, grad_weight)
```

```python
import jax
import jax.numpy as jnp
from jax import lax
from jax.experimental import pallas as pl
from jax.experimental.pallas import tpu as pltpu
from jax.sharding import PartitionSpec as P

loss_scale = 2048.0
beta_value = 2.0

MESH = pl.DeviceIdType.MESH
SIZE = {"z": 8, "y": 4, "x": 4}
BLOB = 11
PARTS = (
    (0, 4, ("y", "z", "x")),
    (4, 8, ("z", "x", "y")),
    (8, 11, ("x", "y", "z")),
)
LANES = 128
TILE = 16
ROWS = 112
TOK = 896
COLS = 512
PAIRS = 16
PAIR = 336
PADDED = 384
F32 = jnp.float32
BF16 = jnp.bfloat16
STEP_US = 1.5
GBS = 45.0e3


def whole(index):
    return slice(None) if index is None else index


class Comm:
    def __init__(self, send_sem, recv_sem):
        self.z = lax.axis_index("section")
        self.y = lax.axis_index("tensor")
        dp = lax.axis_index("dp")
        self.dp = dp
        self.x = dp // 2
        self.c = lax.rem(dp, 2)
        self.send_sem, self.recv_sem = send_sem, recv_sem
        self.used = 0
        self.unsent = []

    def at(self, axis):
        return {"z": self.z, "y": self.y, "x": self.x}[axis]

    def device(self, axis, position):
        z, y, x = self.z, self.y, self.x
        if axis == "z":
            z = position
        elif axis == "y":
            y = position
        else:
            x = position
        return (z, y, 2 * x + self.c)

    def sibling(self):
        return (self.z, self.y, 2 * self.x + 1 - self.c)

    def partner(self):
        return (self.z, self.y + 1 - 2 * lax.rem(self.y, 2), self.dp)

    def send(self, src, dst, device, landing=None):
        i = self.used
        self.used += 1
        copy = pltpu.make_async_remote_copy(
            src_ref=src,
            dst_ref=dst,
            send_sem=self.send_sem.at[i],
            recv_sem=self.recv_sem.at[i],
            device_id=device,
            device_id_type=MESH,
        )
        copy.start()
        self.unsent.append(copy)
        land = dst if landing is None else landing
        return pltpu.make_async_remote_copy(
            src_ref=land,
            dst_ref=land,
            send_sem=self.send_sem.at[i],
            recv_sem=self.recv_sem.at[i],
            device_id=device,
            device_id_type=MESH,
        ).wait_recv

    def drain(self):
        for copy in self.unsent:
            copy.wait_send()
        self.unsent = []


def run(generators, work=(), work_us=0.0):
    now = 0.0
    work = list(work)
    live = []
    for order, gen in enumerate(generators):
        live.append([next(gen), order, gen])
    while live:
        live.sort(key=lambda entry: entry[:2])
        entry = live[0]
        while work and entry[0] > now:
            work.pop(0)()
            now += work_us
        now = max(now, entry[0])
        try:
            entry[0] = now + next(entry[2])
        except StopIteration:
            live.pop(0)
    for item in work:
        item()


def wrap(position, n):
    return lax.rem(position + 2 * n, n)


def slab_index(comm, axis, position, free, lo, hi, half):
    index = {name: None if name in free else comm.at(name) for name in SIZE}
    index[axis] = position
    if half is not None:
        if free:
            name = free[0]
            count = SIZE[name] // 2
            index[name] = pl.ds(half * count, count)
        else:
            middle = lo + (hi - lo + 1) // 2
            lo, hi = (lo, middle) if half == 0 else (middle, hi)
    return tuple(whole(index[name]) for name in ("z", "y", "x")), lo, hi


def slab_bytes(axis, free, lo, hi, itemsize=2):
    count = 1
    for name in free:
        count *= SIZE[name]
    return count * (hi - lo) * TILE * LANES * itemsize


def gather_part(comm, held, lo, hi, order):
    landed = []

    def view(axis, position, free, half, core):
        (zi, yi, xi), a, b = slab_index(comm, axis, position, free, lo, hi, half)
        return held.at[zi, yi, xi, core, a:b]

    for phase, axis in enumerate(order):
        n, me = SIZE[axis], comm.at(axis)
        free = order[:phase]
        last = phase == 2
        right, left = comm.device(axis, wrap(me + 1, n)), comm.device(axis, wrap(me - 1, n))

        def share(position, half, free=free, axis=axis):
            src = view(axis, position, free, half, comm.c)
            landed.append(
                comm.send(src, src, comm.sibling(), landing=view(axis, position, free, half, 1 - comm.c))
            )

        us = slab_bytes(axis, free, lo, hi) / GBS + STEP_US
        for step in range(1, n // 2 + 1):
            ends = step == n // 2
            goes_right, goes_left = wrap(me - step + 1, n), wrap(me + step - 1, n)
            half_right, half_left = (0, 1) if ends else (None, None)
            src = view(axis, goes_right, free, half_right, comm.c)
            wait_left = comm.send(
                src, src, right, landing=view(axis, wrap(me - step, n), free, half_right, comm.c)
            )
            src = view(axis, goes_left, free, half_left, comm.c)
            wait_right = comm.send(
                src, src, left, landing=view(axis, wrap(me + step, n), free, half_left, comm.c)
            )
            if last:
                share(goes_right, None)
                if step > 1:
                    share(goes_left, None)
            yield us * (0.6 if ends else 1.0)
            wait_left()
            wait_right()
        if last:
            share(wrap(me - n // 2, n), 0)
            share(wrap(me + n // 2, n), 1)
    yield 3.0
    for wait in landed:
        wait()


def reduce_shapes():
    shapes = []
    for lo, hi, order in PARTS:
        axes = order[::-1]
        for phase, axis in enumerate(axes):
            free = axes[phase + 1 :]
            for step in range(SIZE[axis] // 2, 0, -1):
                ends = step == SIZE[axis] // 2
                for half in (0, 1):
                    dims = [SIZE[name] for name in ("z", "y", "x") if name in free]
                    tiles = hi - lo
                    if ends:
                        if free:
                            dims = [
                                SIZE[name] // (2 if name == free[0] else 1)
                                for name in ("z", "y", "x")
                                if name in free
                            ]
                        else:
                            tiles = (tiles + 1) // 2 if half == 0 else tiles // 2
                    shapes.append(
                        pltpu.VMEM((*dims, tiles, TILE, LANES), F32 if phase == 2 else BF16)
                    )
        shapes.append(pltpu.VMEM((SIZE[axes[2]], hi - lo, TILE, LANES), F32))
    return shapes


def reduce_part(comm, partial, result, lo, hi, order, buffers):
    axes = order[::-1]
    wide = buffers[-1]
    buffers = list(buffers[:-1])

    for phase, axis in enumerate(axes):
        n, me = SIZE[axis], comm.at(axis)
        free = axes[phase + 1 :]
        last = phase == 2
        right, left = comm.device(axis, wrap(me + 1, n)), comm.device(axis, wrap(me - 1, n))

        def view(position, half):
            if last:
                _, a, b = slab_index(comm, axis, position, (), lo, hi, half)
                return wide.at[position, a - lo : b - lo]
            (zi, yi, xi), a, b = slab_index(comm, axis, position, free, lo, hi, half)
            return partial.at[zi, yi, xi, comm.c, a:b]

        us = slab_bytes(axis, free, lo, hi, 4 if last else 2) / GBS + STEP_US + 0.3
        came = None
        for step in range(n // 2, 0, -1):
            ends = step == n // 2
            if came is not None:
                for side, (buffer, wait, half) in enumerate(came):
                    wait()
                    position = wrap(me + step, n) if side == 0 else wrap(me - step, n)
                    own = view(position, half)
                    total = own[...].astype(F32) + buffer[...].astype(F32)
                    own[...] = total.astype(own.dtype)
            came = []
            for side in (0, 1):
                half = side if ends else None
                position = wrap(me + step, n) if side == 0 else wrap(me - step, n)
                buffer = buffers.pop(0)
                wait = comm.send(view(position, half), buffer, right if side == 0 else left)
                came.append((buffer, wait, half))
            yield us * (0.6 if ends else 1.0)
        for _, wait, _ in came:
            wait()
        own = view(me, None)
        total = own[...].astype(F32) + came[0][0][...].astype(F32) + came[1][0][...].astype(F32)
        if last:
            result[lo:hi] = total
        elif phase == 1:
            wide[...] = total
        else:
            own[...] = total.astype(BF16)


def load_hidden(held, z):
    tiles = []
    for pair in (0, 1):
        even, odd = 2 * pair, 2 * pair + 1
        middle = jnp.concatenate([held[z, even, :, :, 7:11], held[z, odd, :, :, 0:3]], axis=2)
        for part in (held[z, even, :, :, 0:7], middle, held[z, odd, :, :, 3:10]):
            tiles.append(part.reshape(TOK, LANES))
    return jnp.concatenate(tiles, axis=1)


def kernel(
    own_ref, weight_ref, target_ref, onehot_ref, counts_ref, ref_ref, sign_ref, same_ref,
    logprobs_ref, hidden_grad_ref, weight_grad_ref,
    held, partial, padded, logits, dlogits, swap, stats, far, near, final, near_out, swapped,
    send_sem, recv_sem, local_sem, *buffers,
):
    comm = Comm(send_sem, recv_sem)
    even = lax.rem(comm.y, 2) == 0

    def weight_copy(i):
        return pltpu.make_async_copy(
            weight_ref.at[pl.ds(pl.multiple_of(i * PAIR, TILE), PAIR)],
            padded.at[pl.ds(pl.multiple_of(i * PADDED, TILE), PAIR)],
            local_sem.at[i],
        )

    for i in range(PAIRS):
        weight_copy(i).start()

    barrier = pltpu.get_barrier_semaphore()
    peers = []
    for axis, n in (("section", 8), ("tensor", 4), ("dp", 8)):
        me = lax.axis_index(axis)
        for offset in range(1, n):
            place = {"section": comm.z, "tensor": comm.y, "dp": comm.dp}
            place[axis] = lax.rem(me + offset, n)
            peers.append((place["section"], place["tensor"], place["dp"]))
    for peer in peers:
        pl.semaphore_signal(barrier, inc=1, device_id=peer, device_id_type=MESH)
    pl.semaphore_wait(barrier, len(peers))

    wait = comm.send(own_ref.at[1], swap, comm.partner())
    for i in range(PAIRS):
        padded[i * PADDED + PAIR : (i + 1) * PADDED] = jnp.zeros((PADDED - PAIR, COLS), BF16)
    wait()
    shared = own_ref[1] + swap[...]
    zero_tile = jnp.zeros((1, TILE, LANES), BF16)
    held[comm.z, comm.y, comm.x, comm.c] = jnp.where(
        even,
        jnp.concatenate([own_ref[0], shared[0:4]], axis=0),
        jnp.concatenate([shared[4:7], own_ref[0], zero_tile], axis=0),
    )

    run([gather_part(comm, held, lo, hi, order) for lo, hi, order in PARTS])

    for i in range(PAIRS):
        weight_copy(i).wait()

    logits[...] = jnp.zeros_like(logits)

    @pl.loop(0, 8)
    def _(z):
        logits[...] += jnp.dot(
            load_hidden(held, z),
            padded[pl.ds(pl.multiple_of(z * 2 * PADDED, LANES), 2 * PADDED)],
            preferred_element_type=F32,
        )

    first = ((comm.z * 4 + comm.y) * 8 + comm.dp) * COLS
    columns = first + lax.broadcasted_iota(jnp.int32, (LANES, COLS), 1)
    lane = lax.broadcasted_iota(jnp.int32, (LANES, LANES), 1)
    stats[...] = jnp.zeros_like(stats)
    for j in range(TOK // LANES):
        rows = slice(j * LANES, (j + 1) * LANES)
        block = logits[rows]
        top = jnp.max(block, axis=1, keepdims=True)
        total = jnp.sum(jnp.exp(block - top), axis=1, keepdims=True)
        picked = jnp.sum(jnp.where(target_ref[rows] == columns, block, 0.0), axis=1, keepdims=True)
        turned = jnp.where(lane == 0, top, jnp.where(lane == 1, total, picked)).T
        for i in range(3):
            stats[i, j : j + 1] = turned[i : i + 1]

    for axis, n, slots in (("dp", 8, far.at[0]), ("tensor", 4, near), ("section", 8, far.at[1])):
        me = lax.axis_index(axis)
        waits = []
        slots[me] = stats[...]
        for offset in range(1, n):
            place = {"section": comm.z, "tensor": comm.y, "dp": comm.dp}
            place[axis] = lax.rem(me + offset, n)
            waits.append(
                comm.send(
                    slots.at[me],
                    slots.at[me],
                    (place["section"], place["tensor"], place["dp"]),
                    landing=slots.at[lax.rem(me + n - offset, n)],
                )
            )
        for wait in waits:
            wait()
        tops = [slots[i, 0] for i in range(n)]
        top = tops[0]
        for i in range(1, n):
            top = jnp.maximum(top, tops[i])
        total = slots[0, 1] * jnp.exp(tops[0] - top)
        picked = slots[0, 2]
        for i in range(1, n):
            total += slots[i, 1] * jnp.exp(tops[i] - top)
            picked += slots[i, 2]
        stats[0] = top
        stats[1] = total
        stats[2] = picked
        comm.drain()

    log_total = stats[0] + jnp.log(jnp.where(stats[1] > 0.0, stats[1], 1.0))
    terms = stats[2] - log_total
    row = jnp.concatenate([terms[j : j + 1] for j in range(TOK // LANES)], axis=1)
    counts = counts_ref[...]
    sign = sign_ref[...]
    logprobs = jnp.sum(onehot_ref[...] * row, axis=1, keepdims=True) / counts
    logprobs_ref[...] = logprobs
    contrib = sign * (logprobs - ref_ref[...])
    seq = (16, 16)
    eye = lax.broadcasted_iota(jnp.int32, seq, 0) == lax.broadcasted_iota(jnp.int32, seq, 1)
    across = jnp.sum(jnp.where(eye, contrib, 0.0), axis=0, keepdims=True)
    margin = jnp.sum(same_ref[...] * across, axis=1, keepdims=True)
    coefficient = -loss_scale * beta_value * jax.nn.sigmoid(-beta_value * margin) * sign
    token_weight = jnp.sum(onehot_ref[...] * (coefficient / counts), axis=0, keepdims=True)

    for j in range(TOK // LANES):
        rows = slice(j * LANES, (j + 1) * LANES)
        log_column = jnp.broadcast_to(log_total[j : j + 1], (LANES, LANES)).T[:, 0:1]
        weight_column = jnp.broadcast_to(token_weight[:, rows], (LANES, LANES)).T[:, 0:1]
        probs = jnp.exp(logits[rows] - log_column)
        hit = (target_ref[rows] == columns).astype(F32)
        dlogits[rows] = (weight_column * (hit - probs)).astype(BF16)

    def core_copy(z):
        return pltpu.make_async_remote_copy(
            src_ref=partial.at[z, :, :, 1 - comm.c],
            dst_ref=near_out.at[z],
            send_sem=send_sem.at[comm.used + z],
            recv_sem=recv_sem.at[comm.used + z],
            device_id=comm.sibling(),
            device_id_type=MESH,
        )

    @pl.loop(0, 8)
    def _(z):
        for pair in (0, 1):
            terms = lax.dot_general(
                dlogits[...],
                padded[pl.ds(pl.multiple_of((2 * z + pair) * PADDED, LANES), PADDED)],
                (((1,), (1,)), ((), ())),
                preferred_element_type=F32,
            ).astype(BF16)
            left, middle, right = (
                terms[:, i * LANES : (i + 1) * LANES].reshape(4, 2, 7, TILE, LANES) for i in range(3)
            )
            partial[z, 2 * pair, :, :, 0:7] = left
            partial[z, 2 * pair, :, :, 7:11] = middle[:, :, 0:4]
            partial[z, 2 * pair + 1, :, :, 0:3] = middle[:, :, 4:7]
            partial[z, 2 * pair + 1, :, :, 3:10] = right
            partial[z, 2 * pair + 1, :, :, 10:11] = jnp.zeros((4, 2, 1, TILE, LANES), BF16)
        core_copy(z).start()

    @pl.loop(0, 8)
    def _(z):
        core_copy(z).wait()
        for y in range(4):
            mine = partial[z, y, :, comm.c].astype(F32) + near_out[z, y].astype(F32)
            partial[z, y, :, comm.c] = mine.astype(BF16)

    comm.used += 8

    def grad_copy(i):
        return pltpu.make_async_copy(
            padded.at[pl.ds(pl.multiple_of(i * PADDED, TILE), PAIR)],
            weight_grad_ref.at[pl.ds(pl.multiple_of(i * PAIR, TILE), PAIR)],
            local_sem.at[i],
        )

    def weight_grad(z):
        def item():
            features = load_hidden(held, z)
            block = lax.dot_general(
                features, dlogits[...], (((0,), (0,)), ((), ())), preferred_element_type=F32
            )
            padded[z * 2 * PADDED : (z + 1) * 2 * PADDED] = block.astype(BF16)
            grad_copy(2 * z).start()
            grad_copy(2 * z + 1).start()

        return item

    generators, taken = [], 0
    for lo, hi, order in PARTS:
        count = 2 * sum(SIZE[axis] // 2 for axis in order) + 1
        generators.append(
            reduce_part(comm, partial, final, lo, hi, order, buffers[taken : taken + count])
        )
        taken += count
    run(generators, [weight_grad(z) for z in range(8)], 1.0)

    mine = final[...].astype(BF16)
    near_send = swap.at[0:4]
    swap[0:4] = jnp.where(even, mine[7:11], jnp.concatenate([mine[0:3], mine[0:1]], axis=0))
    comm.drain()
    comm.send(near_send, swapped, comm.partner())()
    other = swapped[...]
    hidden_grad_ref[0] = jnp.where(even, mine[0:7], mine[3:10])
    hidden_grad_ref[1] = jnp.where(
        even,
        jnp.concatenate([mine[7:11], other[0:3]], axis=0),
        jnp.concatenate([other, mine[0:3]], axis=0),
    )
    comm.drain()
    for i in range(PAIRS):
        grad_copy(i).wait()


def per_device(hidden, head_weight, targets, response_mask, pair_ids, ref_logprobs):
    even = lax.rem(lax.axis_index("tensor"), 2) == 0
    plain = jnp.pad(hidden, ((0, 0), (0, 88)))
    moved = jnp.pad(hidden, ((0, 0), (40, 48)))
    own = jnp.stack(
        [
            jnp.where(even, plain[:, :LANES], moved[:, LANES:]),
            jnp.where(even, plain[:, LANES:], moved[:, :LANES]),
        ]
    ).reshape(2, 7, TILE, LANES)

    seqs = pair_ids.shape[0]
    mask = response_mask.astype(F32)
    onehot = jnp.where(
        jnp.arange(TOK)[None, :] // (TOK // seqs) == jnp.arange(seqs)[:, None], mask[None, :], 0.0
    )
    counts = jnp.sum(onehot, axis=1, keepdims=True)
    same = pair_ids[:, None] == pair_ids[None, :]
    index = jnp.arange(seqs, dtype=jnp.int32)
    earlier = jnp.sum((same & (index[None, :] < index[:, None])).astype(jnp.int32), axis=1, keepdims=True)
    sign = jnp.where(earlier == 0, 1.0, -1.0).astype(F32)

    vmem = pl.BlockSpec(memory_space=pltpu.VMEM)
    hbm = pl.BlockSpec(memory_space=pl.ANY)
    copies = 160
    logprobs, parts, grad_weight = pl.pallas_call(
        kernel,
        out_shape=(
            jax.ShapeDtypeStruct((seqs, 1), F32),
            jax.ShapeDtypeStruct((2, 7, TILE, LANES), BF16),
            jax.ShapeDtypeStruct(head_weight.shape, BF16),
        ),
        in_specs=[vmem, hbm, vmem, vmem, vmem, vmem, vmem, vmem],
        out_specs=(vmem, vmem, hbm),
        scratch_shapes=[
            pltpu.VMEM((8, 4, 4, 2, BLOB, TILE, LANES), BF16),
            pltpu.VMEM((8, 4, 4, 2, BLOB, TILE, LANES), BF16),
            pltpu.VMEM((PAIRS * PADDED, COLS), BF16),
            pltpu.VMEM((TOK, COLS), F32),
            pltpu.VMEM((TOK, COLS), BF16),
            pltpu.VMEM((7, TILE, LANES), BF16),
            pltpu.VMEM((3, 8, LANES), F32),
            pltpu.VMEM((2, 8, 3, 8, LANES), F32),
            pltpu.VMEM((4, 3, 8, LANES), F32),
            pltpu.VMEM((BLOB, TILE, LANES), F32),
            pltpu.VMEM((8, 4, 4, BLOB, TILE, LANES), BF16),
            pltpu.VMEM((4, TILE, LANES), BF16),
            pltpu.SemaphoreType.DMA((copies,)),
            pltpu.SemaphoreType.DMA((copies,)),
            pltpu.SemaphoreType.DMA((PAIRS,)),
            *reduce_shapes(),
        ],
        compiler_params=pltpu.CompilerParams(
            collective_id=0, has_side_effects=True, vmem_limit_bytes=60 * 1024 * 1024
        ),
        cost_estimate=pl.CostEstimate(
            flops=6 * TOK * 5376 * COLS, bytes_accessed=12 * 1024 * 1024, transcendentals=2 * TOK * COLS
        ),
    )(
        own, head_weight, targets[:, None], onehot, counts, ref_logprobs[:, None], sign, same.astype(F32)
    )

    tile, shared = parts[0].reshape(ROWS, LANES), parts[1].reshape(ROWS, LANES)
    grad_hidden = jnp.where(
        even,
        jnp.concatenate([tile, shared[:, :40]], axis=1),
        jnp.concatenate([shared[:, 40:], tile[:, :80]], axis=1),
    )
    return (logprobs[:, 0], grad_hidden, grad_weight)


def solution(mesh):
    placed = (
        P("dp", ("section", "tensor")),
        P(None, ("section", "tensor", "dp")),
        P(),
        P(),
        P(),
        P(),
    )
    return jax.shard_map(
        per_device,
        mesh=mesh,
        in_specs=placed,
        out_specs=(P(), P("dp", ("section", "tensor")), P(None, ("section", "tensor", "dp"))),
        check_vma=False,
    )
```

```python
import heapq
import itertools

import jax
import jax.numpy as jnp
from jax import lax
from jax.experimental import pallas as pl
from jax.experimental.pallas import tpu as pltpu
from jax.sharding import PartitionSpec as P

loss_scale = 2048.0
beta_value = 2.0

MESH = pl.DeviceIdType.MESH
SIZE = {"z": 8, "y": 4, "x": 4}
BLOB = 11
CUTS = ((0, 5), (5, 9), (9, 11))
LANES = 128
TILE = 16
ROWS = 112
WIDE = 168
TOK = 896
SEQS = 16
SEQ = 56
COLS = 512
PAIRS = 16
PAIR = 336
PADDED = 384
F32 = jnp.float32
BF16 = jnp.bfloat16
HOP_US = 1.5
LINK = 45.0e3
MATMUL_US = 0.8
FAR_FIRST = (4, 3, -3, 2, -2, 1, -1, 0)


class Comm:
    def __init__(self, send_sem, recv_sem):
        self.z = lax.axis_index("section")
        self.y = lax.axis_index("tensor")
        dp = lax.axis_index("dp")
        self.dp = dp
        self.x = dp // 2
        self.c = lax.rem(dp, 2)
        self.send_sem, self.recv_sem = send_sem, recv_sem
        self.used = 0
        self.unsent = []

    def at(self, axis):
        return {"z": self.z, "y": self.y, "x": self.x}[axis]

    def step(self, axis, offset):
        return lax.rem(self.at(axis) + offset + 2 * SIZE[axis], SIZE[axis])

    def device(self, axis, offset):
        z, y, x = self.z, self.y, self.x
        position = self.step(axis, offset)
        if axis == "z":
            z = position
        elif axis == "y":
            y = position
        else:
            x = position
        return (z, y, 2 * x + self.c)

    def sibling(self):
        return (self.z, self.y, 2 * self.x + 1 - self.c)

    def partner(self):
        return (self.z, self.y + 1 - 2 * lax.rem(self.y, 2), self.dp)

    def send(self, src, dst, device, landing=None):
        i = self.used
        self.used += 1
        copy = pltpu.make_async_remote_copy(
            src_ref=src,
            dst_ref=dst,
            send_sem=self.send_sem.at[i],
            recv_sem=self.recv_sem.at[i],
            device_id=device,
            device_id_type=MESH,
        )
        copy.start()
        self.unsent.append(copy)
        land = dst if landing is None else landing
        return pltpu.make_async_remote_copy(
            src_ref=land,
            dst_ref=land,
            send_sem=self.send_sem.at[i],
            recv_sem=self.recv_sem.at[i],
            device_id=device,
            device_id_type=MESH,
        ).wait_recv

    def drain(self):
        for copy in self.unsent:
            copy.wait_send()
        self.unsent = []


class Event:
    def __init__(self):
        self.fired = False
        self.waiting = []


class Timeline:
    def __init__(self):
        self.now = 0.0
        self.heap = []
        self.order = itertools.count()
        self.work = []

    def spawn(self, generator, after=0.0):
        heapq.heappush(self.heap, (self.now + after, next(self.order), generator))

    def fire(self, event):
        event.fired = True
        for generator in event.waiting:
            self.spawn(generator)
        event.waiting = []

    def busy(self, us):
        self.now += us

    def run(self):
        while self.heap:
            while self.work and self.heap[0][0] > self.now + 0.4 * MATMUL_US:
                self.work.pop(0)()
                self.busy(MATMUL_US)
            when, _, generator = heapq.heappop(self.heap)
            self.now = max(self.now, when)
            while True:
                try:
                    wish = next(generator)
                except StopIteration:
                    break
                if isinstance(wish, Event):
                    if wish.fired:
                        continue
                    wish.waiting.append(generator)
                else:
                    self.spawn(generator, wish)
                break
        while self.work:
            self.work.pop(0)()


def copy_us(tiles, itemsize=2):
    return tiles * TILE * LANES * itemsize / LINK + HOP_US


def part_views(comm, array, core):
    (l0, h0), (l1, h1), (l2, h2) = CUTS

    def view0(z, x, half=None):
        y = slice(None) if half is None else pl.ds(2 * half, 2)
        return array.at[z, y, x, core, l0:h0]

    def view1(z, y, half=None):
        x = slice(None) if half is None else pl.ds(2 * half, 2)
        return array.at[z, y, x, core, l1:h1]

    def view2(z, half=None):
        y = slice(None) if half is None else pl.ds(2 * half, 2)
        return array.at[z, y, :, core, l2:h2]

    return view0, view1, view2


def gather(comm, held, line, add_logits):
    view0, view1, view2 = part_views(comm, held, comm.c)
    z0, y0, x0 = comm.z, comm.y, comm.x
    missing = {d: 3 for d in (0, 1, -1, 2, -2, 3, -3, 4)}
    tiles = [hi - lo for lo, hi in CUTS]

    def finish(d):
        missing[d] -= 1
        if missing[d] == 0:
            z = comm.step("z", d)
            src = held.at[z, :, :, comm.c]
            wait = comm.send(src, src, comm.sibling(), landing=held.at[z, :, :, 1 - comm.c])

            def rest():
                yield 3.0
                wait()
                add_logits(z, d)
                line.busy(MATMUL_US)

            line.spawn(rest())

    def ring(axis, view, d, count):
        z = comm.step("z", d)
        me = comm.at(axis)
        src = view(z, me)
        left = comm.send(src, src, comm.device(axis, 1), landing=view(z, comm.step(axis, -1)))
        right = comm.send(src, src, comm.device(axis, -1), landing=view(z, comm.step(axis, 1)))
        yield copy_us(count)
        left()
        right()
        src = view(z, comm.step(axis, -1), 0)
        left = comm.send(src, src, comm.device(axis, 1), landing=view(z, comm.step(axis, 2), 0))
        src = view(z, comm.step(axis, 1), 1)
        right = comm.send(src, src, comm.device(axis, -1), landing=view(z, comm.step(axis, 2), 1))
        yield copy_us(count / 2)
        left()
        right()
        finish(d)

    def along_z(view, count, then):
        for s in (1, 2, 3, 4):
            h0, h1 = (0, 1) if s == 4 else (None, None)
            src = view(comm.step("z", 1 - s), h0)
            left = comm.send(src, src, comm.device("z", 1), landing=view(comm.step("z", -s), h0))
            src = view(comm.step("z", s - 1), h1)
            right = comm.send(src, src, comm.device("z", -1), landing=view(comm.step("z", s), h1))
            if s == 1:
                then(0)
            yield copy_us(count * (0.5 if s == 4 else 1.0))
            left()
            right()
            if s < 4:
                line.spawn(later(then, -s), 0.01)
                line.spawn(later(then, s), 0.01)
        then(4)

    def later(then, d):
        then(d)
        return
        yield

    def start0():
        src = held.at[z0, y0, x0, comm.c, CUTS[0][0] : CUTS[0][1]]
        waits = [
            comm.send(
                src, src, comm.device("y", o),
                landing=held.at[z0, comm.step("y", -o), x0, comm.c, CUTS[0][0] : CUTS[0][1]],
            )
            for o in (1, -1, 2)
        ]
        yield copy_us(3 * tiles[0])
        for wait in waits:
            wait()
        line.spawn(
            along_z(
                lambda z, half=None: view0(z, x0, half),
                4 * tiles[0],
                lambda d: line.spawn(ring("x", view0, d, 4 * tiles[0])),
            )
        )

    def start1():
        lo, hi = CUTS[1][0], CUTS[2][1]
        src = held.at[z0, y0, x0, comm.c, lo:hi]
        waits = [
            comm.send(
                src, src, comm.device("x", o), landing=held.at[z0, y0, comm.step("x", -o), comm.c, lo:hi]
            )
            for o in (1, -1, 2)
        ]
        yield copy_us(3 * (hi - lo))
        for wait in waits:
            wait()
        line.spawn(
            along_z(
                lambda z, half=None: view1(z, y0, half),
                4 * tiles[1],
                lambda d: line.spawn(ring("y", view1, d, 4 * tiles[1])),
            )
        )
        src = held.at[z0, y0, :, comm.c, CUTS[2][0] : CUTS[2][1]]
        waits = [
            comm.send(
                src, src, comm.device("y", o),
                landing=held.at[z0, comm.step("y", -o), :, comm.c, CUTS[2][0] : CUTS[2][1]],
            )
            for o in (1, -1, 2)
        ]
        yield copy_us(3 * 4 * tiles[2])
        for wait in waits:
            wait()
        line.spawn(along_z(view2, 16 * tiles[2], finish))

    line.spawn(start1())
    line.spawn(start0())
    line.run()


def reduce_shapes():
    t0, t1, t2 = (hi - lo for lo, hi in CUTS)
    end = (TILE, LANES)
    shapes = []
    for tiles in (t0, t1):
        shapes += [
            pltpu.VMEM((8, 2, 2, tiles, *end), BF16),
            pltpu.VMEM((8, 2, 4, tiles, *end), BF16),
            pltpu.VMEM((2, 2, tiles, *end), BF16),
            pltpu.VMEM((3, 2, 4, tiles, *end), BF16),
            pltpu.VMEM((4, tiles, *end), F32),
            pltpu.VMEM((3, tiles, *end), F32),
        ]
    shapes += [
        pltpu.VMEM((2, 2, 4, t2, *end), BF16),
        pltpu.VMEM((3, 2, 4, 4, t2, *end), BF16),
        pltpu.VMEM((4, 4, t2, *end), F32),
        pltpu.VMEM((3, 4, t2, *end), F32),
        pltpu.VMEM((4, t2, *end), F32),
        pltpu.VMEM((3, t2, *end), F32),
    ]
    return shapes


def reduce(comm, partial, result, buffers, line, ready):
    view0, view1, view2 = part_views(comm, partial, comm.c)
    tiles = [hi - lo for lo, hi in CUTS]

    def add(own, *others):
        total = own[...].astype(F32)
        for other in others:
            total += other[...].astype(F32)
        own[...] = total.astype(own.dtype)
        line.busy(0.3)

    def ring(axis, view, d, count, halves, fulls, done):
        yield ready[d]
        slot = FAR_FIRST.index(d)
        z = comm.step("z", d)
        left = comm.send(view(z, comm.step(axis, 2), 0), halves.at[slot, 0], comm.device(axis, 1))
        right = comm.send(view(z, comm.step(axis, 2), 1), halves.at[slot, 1], comm.device(axis, -1))
        yield copy_us(count / 2)
        left()
        add(view(z, comm.step(axis, 1), 0), halves.at[slot, 0])
        left = comm.send(view(z, comm.step(axis, 1)), fulls.at[slot, 0], comm.device(axis, 1))
        right()
        add(view(z, comm.step(axis, -1), 1), halves.at[slot, 1])
        right = comm.send(view(z, comm.step(axis, -1)), fulls.at[slot, 1], comm.device(axis, -1))
        yield copy_us(count)
        left()
        right()
        add(view(z, comm.at(axis)), fulls.at[slot, 0], fulls.at[slot, 1])
        line.fire(done[d])

    def along_z(view, count, halves, fulls, total, done):
        yield done[4]
        left = comm.send(view(comm.step("z", 4), 0), halves.at[0], comm.device("z", 1))
        right = comm.send(view(comm.step("z", 4), 1), halves.at[1], comm.device("z", -1))
        came = (halves.at[0], halves.at[1])
        yield copy_us(count / 2)
        for s in (3, 2, 1):
            yield done[s]
            left()
            add(view(comm.step("z", s), 0 if s == 3 else None), came[0])
            left = comm.send(view(comm.step("z", s)), fulls.at[s - 1, 0], comm.device("z", 1))
            yield done[-s]
            right()
            add(view(comm.step("z", -s), 1 if s == 3 else None), came[1])
            right = comm.send(view(comm.step("z", -s)), fulls.at[s - 1, 1], comm.device("z", -1))
            came = (fulls.at[s - 1, 0], fulls.at[s - 1, 1])
            yield copy_us(count)
        yield done[0]
        left()
        right()
        total[...] = view(comm.z)[...].astype(F32) + came[0][...].astype(F32) + came[1][...].astype(F32)
        line.busy(0.3)

    def direct(axis, source, landing, count):
        waits = [
            comm.send(source.at[comm.step(axis, o)], landing.at[k], comm.device(axis, o))
            for k, o in enumerate((1, -1, 2))
        ]
        yield copy_us(3 * count, 4)
        for wait in waits:
            wait()

    def place(axis, source, landing, lo, hi):
        result[lo:hi] = source[comm.at(axis)] + landing[0] + landing[1] + landing[2]

    def side(axis, last, view, fixed, cut, bufs):
        halves, fulls, z_halves, z_fulls, total, landing = bufs
        count = 4 * (cut[1] - cut[0])
        done = {d: Event() for d in FAR_FIRST}
        for d in FAR_FIRST:
            line.spawn(ring(axis, view, d, count, halves, fulls, done))

        def rest():
            yield from along_z(
                lambda z, half=None: view(z, fixed, half), count, z_halves, z_fulls, total, done
            )
            yield from direct(last, total, landing, cut[1] - cut[0])
            place(last, total, landing, *cut)

        line.spawn(rest())

    side("x", "y", view0, comm.x, CUTS[0], buffers[0:6])
    side("y", "x", view1, comm.y, CUTS[1], buffers[6:12])

    def third():
        halves, fulls, total, landing, row, last = buffers[12:18]
        yield from along_z(view2, 16 * tiles[2], halves, fulls, total, ready)
        yield from direct("y", total, landing, 4 * tiles[2])
        row[...] = total[comm.y] + landing[0] + landing[1] + landing[2]
        yield from direct("x", row, last, tiles[2])
        place("x", row, last, *CUTS[2])

    line.spawn(third())


def load_hidden(held, z):
    tiles = []
    for pair in (0, 1):
        even, odd = 2 * pair, 2 * pair + 1
        middle = jnp.concatenate([held[z, even, :, :, 7:11], held[z, odd, :, :, 0:3]], axis=2)
        for part in (held[z, even, :, :, 0:7], middle, held[z, odd, :, :, 3:10]):
            tiles.append(part.reshape(TOK, LANES))
    return jnp.concatenate(tiles, axis=1)


def selection(odd):
    feature = lax.broadcasted_iota(jnp.int32, (WIDE, 2 * LANES), 0)
    place = lax.broadcasted_iota(jnp.int32, (WIDE, 2 * LANES), 1)
    return (place == feature + 40 * odd).astype(F32).astype(BF16)


def kernel(
    pair_ref, ref_ref, own_ref, weight_ref, target_ref, mask_ref,
    logprobs_ref, hidden_grad_ref, weight_grad_ref,
    held, partial, padded, logits, dlogits, shared_out, shared_in, stats, far, near, final, near_out, swapped,
    send_sem, recv_sem, local_sem, *buffers,
):
    comm = Comm(send_sem, recv_sem)
    odd = lax.rem(comm.y, 2)
    even = odd == 0

    barrier = pltpu.get_barrier_semaphore()
    peers = []
    for axis, n in (("section", 8), ("tensor", 4), ("dp", 8)):
        me = lax.axis_index(axis)
        for offset in range(1, n):
            place = {"section": comm.z, "tensor": comm.y, "dp": comm.dp}
            place[axis] = lax.rem(me + offset, n)
            peers.append((place["section"], place["tensor"], place["dp"]))
    for peer in peers:
        pl.semaphore_signal(barrier, inc=1, device_id=peer, device_id_type=MESH)

    def weight_copy(i):
        return pltpu.make_async_copy(
            weight_ref.at[pl.ds(pl.multiple_of(i * PAIR, TILE), PAIR)],
            padded.at[pl.ds(pl.multiple_of(i * PADDED, TILE), PAIR)],
            local_sem.at[i],
        )

    for i in range(PAIRS):
        weight_copy(i).start()

    spread = lax.dot_general(
        own_ref[...], selection(odd), (((0,), (0,)), ((), ())), preferred_element_type=F32
    ).astype(BF16)
    low, high = spread[:, :LANES], spread[:, LANES:]
    alone = jnp.where(even, low, high).reshape(7, TILE, LANES)
    shared_out[...] = jnp.where(even, high, low).reshape(7, TILE, LANES)
    pl.semaphore_wait(barrier, len(peers))

    wait = comm.send(shared_out, shared_in, comm.partner())
    for i in range(PAIRS):
        padded[i * PADDED + PAIR : (i + 1) * PADDED] = jnp.zeros((PADDED - PAIR, COLS), BF16)
    logits[...] = jnp.zeros_like(logits)
    wait()
    shared = shared_out[...] + shared_in[...]
    zero_tile = jnp.zeros((1, TILE, LANES), BF16)
    held[comm.z, comm.y, comm.x, comm.c] = jnp.where(
        even,
        jnp.concatenate([alone, shared[0:4]], axis=0),
        jnp.concatenate([shared[4:7], alone, zero_tile], axis=0),
    )

    def add_logits(z, d):
        if d == 0:
            for i in range(PAIRS):
                weight_copy(i).wait()
        logits[...] += jnp.dot(
            load_hidden(held, z),
            padded[pl.ds(pl.multiple_of(z * 2 * PADDED, LANES), 2 * PADDED)],
            preferred_element_type=F32,
        )

    line = Timeline()
    gather(comm, held, line, add_logits)

    def column(row):
        return jnp.broadcast_to(row, (LANES, LANES)).T[:, 0:1]

    def target_column(j):
        return column(target_ref[j : j + 1].astype(F32))

    first = ((comm.z * 4 + comm.y) * 8 + comm.dp) * COLS
    columns = first + lax.broadcasted_iota(jnp.int32, (LANES, COLS), 1)
    columns = columns.astype(F32)
    lane = lax.broadcasted_iota(jnp.int32, (LANES, LANES), 1)
    stats[...] = jnp.zeros_like(stats)
    for j in range(TOK // LANES):
        rows = slice(j * LANES, (j + 1) * LANES)
        block = logits[rows]
        top = jnp.max(block, axis=1, keepdims=True)
        total = jnp.sum(jnp.exp(block - top), axis=1, keepdims=True)
        picked = jnp.sum(jnp.where(target_column(j) == columns, block, 0.0), axis=1, keepdims=True)
        turned = jnp.where(lane == 0, top, jnp.where(lane == 1, total, picked)).T
        for i in range(3):
            stats[i, j : j + 1] = turned[i : i + 1]

    for axis, n, slots in (("dp", 8, far.at[0]), ("tensor", 4, near), ("section", 8, far.at[1])):
        me = lax.axis_index(axis)
        waits = []
        slots[me] = stats[...]
        for offset in range(1, n):
            place = {"section": comm.z, "tensor": comm.y, "dp": comm.dp}
            place[axis] = lax.rem(me + offset, n)
            waits.append(
                comm.send(
                    slots.at[me],
                    slots.at[me],
                    (place["section"], place["tensor"], place["dp"]),
                    landing=slots.at[lax.rem(me + n - offset, n)],
                )
            )
        for wait in waits:
            wait()
        tops = [slots[i, 0] for i in range(n)]
        top = tops[0]
        for i in range(1, n):
            top = jnp.maximum(top, tops[i])
        total = slots[0, 1] * jnp.exp(tops[0] - top)
        picked = slots[0, 2]
        for i in range(1, n):
            total += slots[i, 1] * jnp.exp(tops[i] - top)
            picked += slots[i, 2]
        stats[0] = top
        stats[1] = total
        stats[2] = picked
        comm.drain()

    log_total = stats[0] + jnp.log(jnp.where(stats[1] > 0.0, stats[1], 1.0))
    terms = stats[2] - log_total

    def flat(rows):
        return jnp.concatenate([rows[j : j + 1] for j in range(TOK // LANES)], axis=1)

    token = lax.broadcasted_iota(jnp.int32, (SEQS, TOK), 1)
    start = SEQ * lax.broadcasted_iota(jnp.int32, (SEQS, TOK), 0)
    onehot = jnp.where((token >= start) & (token < start + SEQ), flat(mask_ref[...].astype(F32)), 0.0)
    counts = jnp.sum(onehot, axis=1, keepdims=True)
    seq = (SEQS, SEQS)
    down, right = lax.broadcasted_iota(jnp.int32, seq, 0), lax.broadcasted_iota(jnp.int32, seq, 1)
    pair_down, pair_right = jnp.zeros(seq, jnp.int32), jnp.zeros(seq, jnp.int32)
    ref_down = jnp.zeros(seq, F32)
    for i in range(SEQS):
        pair_down = jnp.where(down == i, pair_ref[i], pair_down)
        pair_right = jnp.where(right == i, pair_ref[i], pair_right)
        ref_down = jnp.where(down == i, ref_ref[i], ref_down)
    same = jnp.where(pair_down == pair_right, 1.0, 0.0)
    earlier = jnp.sum(jnp.where(right < down, same, 0.0), axis=1, keepdims=True)
    sign = jnp.where(earlier == 0.0, 1.0, -1.0)
    eye = down == right

    logprobs = jnp.sum(onehot * flat(terms), axis=1, keepdims=True) / counts
    logprobs_ref[...] = jnp.sum(jnp.where(eye, logprobs, 0.0), axis=0, keepdims=True)
    contrib = sign * (logprobs - ref_down[:, 0:1])
    across = jnp.sum(jnp.where(eye, contrib, 0.0), axis=0, keepdims=True)
    margin = jnp.sum(same * across, axis=1, keepdims=True)
    coefficient = -loss_scale * beta_value * jax.nn.sigmoid(-beta_value * margin) * sign
    token_weight = jnp.sum(onehot * (coefficient / counts), axis=0, keepdims=True)

    for j in range(TOK // LANES):
        rows = slice(j * LANES, (j + 1) * LANES)
        probs = jnp.exp(logits[rows] - column(log_total[j : j + 1]))
        hit = (target_column(j) == columns).astype(F32)
        dlogits[rows] = (column(token_weight[:, rows]) * (hit - probs)).astype(BF16)

    line = Timeline()
    ready = {d: Event() for d in FAR_FIRST}

    def hidden_grad(d):
        z = comm.step("z", d)
        for pair in (0, 1):
            terms = lax.dot_general(
                dlogits[...],
                padded[pl.ds(pl.multiple_of((2 * z + pair) * PADDED, LANES), PADDED)],
                (((1,), (1,)), ((), ())),
                preferred_element_type=F32,
            ).astype(BF16)
            left, middle, right = (
                terms[:, i * LANES : (i + 1) * LANES].reshape(4, 2, 7, TILE, LANES) for i in range(3)
            )
            partial[z, 2 * pair, :, :, 0:7] = left
            partial[z, 2 * pair, :, :, 7:11] = middle[:, :, 0:4]
            partial[z, 2 * pair + 1, :, :, 0:3] = middle[:, :, 4:7]
            partial[z, 2 * pair + 1, :, :, 3:10] = right
            partial[z, 2 * pair + 1, :, :, 10:11] = jnp.zeros((4, 2, 1, TILE, LANES), BF16)
        wait = comm.send(partial.at[z, :, :, 1 - comm.c], near_out.at[FAR_FIRST.index(d)], comm.sibling())

        def rest():
            yield 3.0
            wait()
            for y in range(4):
                mine = partial[z, y, :, comm.c].astype(F32) + near_out[FAR_FIRST.index(d), y].astype(F32)
                partial[z, y, :, comm.c] = mine.astype(BF16)
            line.busy(0.3)
            line.fire(ready[d])

        line.spawn(rest())

    def grad_copy(i):
        return pltpu.make_async_copy(
            padded.at[pl.ds(pl.multiple_of(i * PADDED, TILE), PAIR)],
            weight_grad_ref.at[pl.ds(pl.multiple_of(i * PAIR, TILE), PAIR)],
            local_sem.at[i],
        )

    def weight_grad(z):
        def item():
            block = lax.dot_general(
                load_hidden(held, z), dlogits[...], (((0,), (0,)), ((), ())), preferred_element_type=F32
            )
            padded[z * 2 * PADDED : (z + 1) * 2 * PADDED] = block.astype(BF16)
            grad_copy(2 * z).start()
            grad_copy(2 * z + 1).start()

        return item

    def compute():
        for d in FAR_FIRST:
            hidden_grad(d)
            line.busy(MATMUL_US)
            yield 0.0
        line.work = [weight_grad(z) for z in range(8)]

    line.spawn(compute())
    reduce(comm, partial, final, buffers, line, ready)
    line.run()

    mine = final[...].astype(BF16)
    comm.drain()
    shared_out[0:4] = jnp.where(even, mine[7:11], jnp.concatenate([mine[0:3], mine[0:1]], axis=0))
    comm.send(shared_out.at[0:4], swapped, comm.partner())()
    other = swapped[...]
    alone = jnp.where(even, mine[0:7], mine[3:10]).reshape(ROWS, LANES)
    shared = jnp.where(
        even,
        jnp.concatenate([mine[7:11], other[0:3]], axis=0),
        jnp.concatenate([other, mine[0:3]], axis=0),
    ).reshape(ROWS, LANES)
    both = jnp.concatenate([jnp.where(even, alone, shared), jnp.where(even, shared, alone)], axis=1)
    hidden_grad_ref[...] = lax.dot_general(
        selection(odd), both, (((1,), (1,)), ((), ())), preferred_element_type=F32
    ).astype(BF16)
    comm.drain()
    for i in range(PAIRS):
        grad_copy(i).wait()


def per_device(hidden, head_weight, targets, response_mask, pair_ids, ref_logprobs):
    vmem = pl.BlockSpec(memory_space=pltpu.VMEM)
    smem = pl.BlockSpec(memory_space=pltpu.SMEM)
    hbm = pl.BlockSpec(memory_space=pl.ANY)
    copies = 320
    logprobs, turned, grad_weight = pl.pallas_call(
        kernel,
        out_shape=(
            jax.ShapeDtypeStruct((1, SEQS), F32),
            jax.ShapeDtypeStruct((WIDE, ROWS), BF16),
            jax.ShapeDtypeStruct(head_weight.shape, BF16),
        ),
        in_specs=[smem, smem, vmem, hbm, vmem, vmem],
        out_specs=(vmem, vmem, hbm),
        scratch_shapes=[
            pltpu.VMEM((8, 4, 4, 2, BLOB, TILE, LANES), BF16),
            pltpu.VMEM((8, 4, 4, 2, BLOB, TILE, LANES), BF16),
            pltpu.VMEM((PAIRS * PADDED, COLS), BF16),
            pltpu.VMEM((TOK, COLS), F32),
            pltpu.VMEM((TOK, COLS), BF16),
            pltpu.VMEM((7, TILE, LANES), BF16),
            pltpu.VMEM((7, TILE, LANES), BF16),
            pltpu.VMEM((3, 8, LANES), F32),
            pltpu.VMEM((2, 8, 3, 8, LANES), F32),
            pltpu.VMEM((4, 3, 8, LANES), F32),
            pltpu.VMEM((BLOB, TILE, LANES), F32),
            pltpu.VMEM((8, 4, 4, BLOB, TILE, LANES), BF16),
            pltpu.VMEM((4, TILE, LANES), BF16),
            pltpu.SemaphoreType.DMA((copies,)),
            pltpu.SemaphoreType.DMA((copies,)),
            pltpu.SemaphoreType.DMA((PAIRS,)),
            *reduce_shapes(),
        ],
        compiler_params=pltpu.CompilerParams(
            collective_id=0, has_side_effects=True, vmem_limit_bytes=60 * 1024 * 1024
        ),
        cost_estimate=pl.CostEstimate(
            flops=6 * TOK * 5376 * COLS, bytes_accessed=12 * 1024 * 1024, transcendentals=2 * TOK * COLS
        ),
    )(
        pair_ids, ref_logprobs, hidden.T, head_weight,
        targets.reshape(TOK // LANES, LANES), response_mask.reshape(TOK // LANES, LANES),
    )
    return (logprobs.reshape(SEQS), turned.T, grad_weight)


def solution(mesh):
    placed = (
        P("dp", ("section", "tensor")),
        P(None, ("section", "tensor", "dp")),
        P(),
        P(),
        P(),
        P(),
    )
    return jax.shard_map(
        per_device,
        mesh=mesh,
        in_specs=placed,
        out_specs=(P(), P("dp", ("section", "tensor")), P(None, ("section", "tensor", "dp"))),
        check_vma=False,
    )
```

```python
import heapq
import itertools
import math

import jax
import jax.numpy as jnp
from jax import lax
from jax.experimental import pallas as pl
from jax.experimental.pallas import tpu as pltpu
from jax.sharding import PartitionSpec as P

loss_scale = 2048.0
beta_value = 2.0

MESH = pl.DeviceIdType.MESH
SIZE = {"z": 8, "y": 4, "x": 4}
BLOB = 11
CUTS = ((0, 4), (4, 8), (8, 11))
LANES = 128
TILE = 16
ROWS = 112
WIDE = 168
TOK = 896
SEQS = 16
SEQ = 56
COLS = 512
PAIRS = 16
PAIR = 336
PADDED = 384
F32 = jnp.float32
BF16 = jnp.bfloat16
ISSUE_US = 0.05
HOP_US = 1.5
EACH_HOP_US = 0.5
LINK = 45.0e3
CORE_LINK = 600.0e3
MATMUL_US = 0.8
ADD_US = 0.06
FAR_FIRST = (4, 3, -3, 2, -2, 1, -1, 0)


class Comm:
    def __init__(self, send_sem, recv_sem):
        self.z = lax.axis_index("section")
        self.y = lax.axis_index("tensor")
        dp = lax.axis_index("dp")
        self.dp = dp
        self.x = dp // 2
        self.c = lax.rem(dp, 2)
        self.send_sem, self.recv_sem = send_sem, recv_sem
        self.used = 0
        self.unsent = []
        self.line = Timeline()

    def at(self, axis):
        return {"z": self.z, "y": self.y, "x": self.x}[axis]

    def step(self, axis, offset):
        return lax.rem(self.at(axis) + offset + 2 * SIZE[axis], SIZE[axis])

    def device(self, axis, offset):
        z, y, x = self.z, self.y, self.x
        position = self.step(axis, offset)
        if axis == "z":
            z = position
        elif axis == "y":
            y = position
        else:
            x = position
        return (z, y, 2 * x + self.c)

    def sibling(self):
        return (self.z, self.y, 2 * self.x + 1 - self.c)

    def partner(self):
        return (self.z, self.y + 1 - 2 * lax.rem(self.y, 2), self.dp)

    def send(self, src, dst, axis, offset=None, landing=None):
        i = self.used
        self.used += 1
        if offset is None:
            device = axis
        else:
            device = self.sibling() if axis == "c" else self.device(axis, offset)
        copy = pltpu.make_async_remote_copy(
            src_ref=src,
            dst_ref=dst,
            send_sem=self.send_sem.at[i],
            recv_sem=self.recv_sem.at[i],
            device_id=device,
            device_id_type=MESH,
        )
        copy.start()
        self.unsent.append(copy)
        land = dst if landing is None else landing
        back = pltpu.make_async_remote_copy(
            src_ref=land,
            dst_ref=land,
            send_sem=self.send_sem.at[i],
            recv_sem=self.recv_sem.at[i],
            device_id=device,
            device_id_type=MESH,
        )
        size = math.prod(src.shape) * jnp.dtype(src.dtype).itemsize
        return Landing(self.line, back, self.line.now if offset is None else self.line.carry(axis, offset, size))

    def drain(self):
        for copy in self.unsent:
            copy.wait_send()
        self.unsent = []


class Event:
    def __init__(self):
        self.fired = False
        self.waiting = []


class Landing:
    def __init__(self, line, copy, when):
        self.line, self.copy, self.when = line, copy, when

    def __call__(self):
        self.copy.wait_recv()
        self.line.now = max(self.line.now, self.when)


class Timeline:
    def __init__(self):
        self.now = 0.0
        self.heap = []
        self.order = itertools.count()
        self.work = []
        self.free = {}

    def spawn(self, generator, when=0.0):
        heapq.heappush(self.heap, (max(self.now, when), next(self.order), generator))

    def fire(self, event):
        event.fired = True
        for generator in event.waiting:
            self.spawn(generator)
        event.waiting = []

    def busy(self, us):
        self.now += us

    def carry(self, axis, offset, size):
        self.busy(ISSUE_US)
        link = (axis, offset > 0)
        hops = 1 if axis == "c" else abs(offset)
        us = size / CORE_LINK if axis == "c" else hops * size / LINK
        end = max(self.now, self.free.get(link, 0.0)) + us
        self.free[link] = end
        return end + HOP_US + (EACH_HOP_US * (hops + 1) if axis != "c" else EACH_HOP_US)

    def run(self):
        while self.heap:
            while self.work and self.heap[0][0] > self.now + 0.4 * MATMUL_US:
                self.work.pop(0)()
                self.busy(MATMUL_US)
            when, _, generator = heapq.heappop(self.heap)
            self.now = max(self.now, when)
            while True:
                try:
                    wish = next(generator)
                except StopIteration:
                    break
                if isinstance(wish, Event):
                    if wish.fired:
                        continue
                    wish.waiting.append(generator)
                else:
                    self.spawn(generator, max([landing.when for landing in wish], default=0.0))
                break
        while self.work:
            self.work.pop(0)()
            self.busy(MATMUL_US)


NEAR_FIRST = (1, -1, 2, -2, 3, -3, 4)


def ring_views(comm, array):
    core = comm.c
    (l0, h0), (l1, h1), _ = CUTS

    def cut(lo, hi, half):
        middle = (lo + hi) // 2
        return slice(lo, hi) if half is None else slice(lo, middle) if half == 0 else slice(middle, hi)

    def some(half):
        return slice(None) if half is None else pl.ds(2 * half, 2)

    return (
        (
            ("y", lambda z, y, half=None: array.at[z, y, comm.x, core, cut(l0, h0, half)]),
            ("x", lambda z, x, half=None: array.at[z, some(half), x, core, l0:h0]),
        ),
        (
            ("x", lambda z, x, half=None: array.at[z, comm.y, x, core, cut(l1, h1, half)]),
            ("y", lambda z, y, half=None: array.at[z, y, some(half), core, l1:h1]),
        ),
    )


def third_view(comm, array):
    lo, hi = CUTS[2]

    def view(z, y, half=None):
        return array.at[z, y, slice(None) if half is None else pl.ds(2 * half, 2), comm.c, lo:hi]

    return view


def gather(comm, held, line, add_logits):
    place = (comm.z, comm.y, comm.x, comm.c)
    missing = {d: 6 for d in FAR_FIRST}

    def finish(d):
        missing[d] -= 1
        if missing[d] == 0:
            z = comm.step("z", d)
            src = held.at[z, :, :, comm.c]
            wait = comm.send(src, src, "c", 1, landing=held.at[z, :, :, 1 - comm.c])

            def rest():
                yield [wait]
                wait()
                add_logits(z, d)
                line.busy(MATMUL_US)

            line.spawn(rest())

    def ring(axis, view, d):
        z = comm.step("z", d)
        src = view(z, comm.at(axis))
        left = comm.send(src, src, axis, 1, landing=view(z, comm.step(axis, -1)))
        right = comm.send(src, src, axis, -1, landing=view(z, comm.step(axis, 1)))
        yield [left]
        left()
        src = view(z, comm.step(axis, -1), 0)
        left = comm.send(src, src, axis, 1, landing=view(z, comm.step(axis, 2), 0))
        yield [right]
        right()
        src = view(z, comm.step(axis, 1), 1)
        right = comm.send(src, src, axis, -1, landing=view(z, comm.step(axis, 2), 1))
        yield [left, right]
        left()
        right()

    def chain(rings, d, wait=None):
        if wait is not None:
            yield [wait]
            wait()
        for axis, view in rings:
            yield from ring(axis, view, d)
        finish(d)

    views = ring_views(comm, held)
    first = slice(CUTS[0][0], CUTS[1][1])

    def arrive(d, wait):
        yield [wait]
        wait()
        for rings in views:
            line.spawn(chain(rings, d))

    def along_z(y):
        third = third_view(comm, held)
        for s in (1, 2, 3, 4):
            h0, h1 = (0, 1) if s == 4 else (None, None)
            src = third(comm.step("z", 1 - s), y, h0)
            left = comm.send(src, src, "z", 1, landing=third(comm.step("z", -s), y, h0))
            src = third(comm.step("z", s - 1), y, h1)
            right = comm.send(src, src, "z", -1, landing=third(comm.step("z", s), y, h1))
            if s == 1:
                finish(0)
            yield [left, right]
            left()
            right()
            if s < 4:
                finish(-s)
                finish(s)
        finish(4)

    def start_third():
        lo, hi = CUTS[2]
        src = held.at[(*place, slice(lo, hi))]
        waits = [
            comm.send(
                src, src, "x", o, landing=held.at[comm.z, comm.y, comm.step("x", -o), comm.c, lo:hi]
            )
            for o in (1, -1, 2)
        ]
        yield waits
        for wait in waits:
            wait()
        third = third_view(comm, held)
        src = third(comm.z, comm.y)
        waits = [
            comm.send(src, src, "y", o, landing=third(comm.z, comm.step("y", -o))) for o in (1, -1, 2)
        ]
        line.spawn(along_z(comm.y))
        for wait, o in zip(waits, (1, -1, 2)):
            yield [wait]
            wait()
            line.spawn(along_z(comm.step("y", -o)))

    line.spawn(start_third())
    for rings in views:
        line.spawn(chain(rings, 0))

    def spread():
        src = held.at[(*place, first)]
        for o in NEAR_FIRST:
            landing = held.at[comm.step("z", -o), comm.y, comm.x, comm.c, first]
            wait = comm.send(src, src, "z", o, landing=landing)
            line.spawn(arrive(4 if o == 4 else -o, wait))
        return
        yield

    line.spawn(spread())
    line.run()


def reduce_shapes():
    t0, t1, t2 = (hi - lo for lo, hi in CUTS)
    end = (TILE, LANES)
    shapes = []
    for tiles in (t0, t1):
        shapes += [
            pltpu.VMEM((8, 2, 2, tiles, *end), BF16),
            pltpu.VMEM((8, 2, 4, tiles, *end), BF16),
            pltpu.VMEM((8, 2, tiles // 2, *end), BF16),
            pltpu.VMEM((8, 2, tiles, *end), BF16),
            pltpu.VMEM((7, tiles, *end), BF16),
        ]
    shapes += [
        pltpu.VMEM((4, 2, 2, t2, *end), BF16),
        pltpu.VMEM((4, 3, 2, 4, t2, *end), BF16),
        pltpu.VMEM((3, 4, t2, *end), BF16),
        pltpu.VMEM((4, t2, *end), F32),
        pltpu.VMEM((3, t2, *end), F32),
    ]
    return shapes


def reduce(comm, partial, result, buffers, line, ready):
    def add(own, *others):
        if len(others) == 1:
            own[...] = own[...] + others[0][...]
            line.busy(ADD_US)
            return
        total = own[...].astype(F32)
        for other in others:
            total += other[...].astype(F32)
        own[...] = total.astype(own.dtype)
        line.busy(ADD_US)

    def ring(axis, view, d, halves, fulls):
        slot = FAR_FIRST.index(d)
        z = comm.step("z", d)
        left = comm.send(view(z, comm.step(axis, 2), 0), halves.at[slot, 0], axis, 1)
        right = comm.send(view(z, comm.step(axis, 2), 1), halves.at[slot, 1], axis, -1)
        yield [left]
        left()
        add(view(z, comm.step(axis, 1), 0), halves.at[slot, 0])
        left = comm.send(view(z, comm.step(axis, 1)), fulls.at[slot, 0], axis, 1)
        yield [right]
        right()
        add(view(z, comm.step(axis, -1), 1), halves.at[slot, 1])
        right = comm.send(view(z, comm.step(axis, -1)), fulls.at[slot, 1], axis, -1)
        yield [left, right]
        left()
        right()
        add(view(z, comm.at(axis)), fulls.at[slot, 0], fulls.at[slot, 1])

    def side(rings, cut, bufs):
        (near, single), (wide, four) = rings
        landing = bufs[4]
        waits = []
        gate = Event()
        left = [8]

        def chain(d):
            yield ready[d]
            yield from ring(wide, four, d, bufs[0], bufs[1])
            yield from ring(near, single, d, bufs[2], bufs[3])
            if d:
                waits.append(
                    comm.send(single(comm.step("z", d), comm.at(near)), landing.at[len(waits)], "z", d)
                )
            left[0] -= 1
            if left[0] == 0:
                line.fire(gate)

        def rest():
            yield gate
            yield list(waits)
            for wait in waits:
                wait()
            total = single(comm.z, comm.at(near))[...].astype(F32)
            for i in range(7):
                total += landing[i].astype(F32)
            result[cut[0] : cut[1]] = total
            line.busy(ADD_US)

        for d in FAR_FIRST:
            line.spawn(chain(d))
        line.spawn(rest())

    views = ring_views(comm, partial)
    third = third_view(comm, partial)
    halves, fulls, landing, row, last = buffers[10:15]
    waits = []

    def along_z(slot, o):
        y = comm.step("y", o)
        yield ready[4]
        left = comm.send(third(comm.step("z", 4), y, 0), halves.at[slot, 0], "z", 1)
        right = comm.send(third(comm.step("z", 4), y, 1), halves.at[slot, 1], "z", -1)
        came = (halves.at[slot, 0], halves.at[slot, 1])
        for s in (3, 2, 1):
            yield ready[s]
            yield [left]
            left()
            add(third(comm.step("z", s), y, 0 if s == 3 else None), came[0])
            left = comm.send(third(comm.step("z", s), y), fulls.at[slot, s - 1, 0], "z", 1)
            yield ready[-s]
            yield [right]
            right()
            add(third(comm.step("z", -s), y, 1 if s == 3 else None), came[1])
            right = comm.send(third(comm.step("z", -s), y), fulls.at[slot, s - 1, 1], "z", -1)
            came = (fulls.at[slot, s - 1, 0], fulls.at[slot, s - 1, 1])
        yield ready[0]
        yield [left, right]
        left()
        right()
        mine = third(comm.z, y)
        if o:
            add(mine, *came)
            waits.append(comm.send(mine, landing.at[slot], "y", o))
        else:
            row[...] = mine[...].astype(F32) + came[0][...].astype(F32) + came[1][...].astype(F32)
            line.busy(ADD_US)

    gate = Event()
    pending = [4]

    def one(slot, o):
        yield from along_z(slot, o)
        pending[0] -= 1
        if pending[0] == 0:
            line.fire(gate)

    def rest():
        yield gate
        yield list(waits)
        for wait in waits:
            wait()
        total = row[...]
        for i in range(3):
            total += landing[i].astype(F32)
        row[...] = total
        line.busy(ADD_US)
        ends = [comm.send(row.at[comm.step("x", o)], last.at[k], "x", o) for k, o in enumerate((1, -1, 2))]
        yield ends
        for wait in ends:
            wait()
        result[CUTS[2][0] : CUTS[2][1]] = row[comm.x] + last[0] + last[1] + last[2]

    for slot, o in enumerate((2, 1, -1, 0)):
        line.spawn(one(slot, o))
    side(views[0], CUTS[0], buffers[0:5])
    side(views[1], CUTS[1], buffers[5:10])
    line.spawn(rest())


def load_hidden(held, z):
    tiles = []
    for pair in (0, 1):
        even, odd = 2 * pair, 2 * pair + 1
        middle = jnp.concatenate([held[z, even, :, :, 7:11], held[z, odd, :, :, 0:3]], axis=2)
        for part in (held[z, even, :, :, 0:7], middle, held[z, odd, :, :, 3:10]):
            tiles.append(part.reshape(TOK, LANES))
    return jnp.concatenate(tiles, axis=1)


def selection(odd):
    feature = lax.broadcasted_iota(jnp.int32, (WIDE, 2 * LANES), 0)
    place = lax.broadcasted_iota(jnp.int32, (WIDE, 2 * LANES), 1)
    return (place == feature + 40 * odd).astype(F32).astype(BF16)


def kernel(
    pair_ref, ref_ref, own_ref, weight_ref, target_ref, mask_ref,
    logprobs_ref, hidden_grad_ref, weight_grad_ref,
    held, partial, padded, logits, dlogits, shared_out, shared_in, stats, far, near, final, near_out, swapped,
    send_sem, recv_sem, local_sem, *buffers,
):
    comm = Comm(send_sem, recv_sem)
    odd = lax.rem(comm.y, 2)
    even = odd == 0

    barrier = pltpu.get_barrier_semaphore()
    peers = []
    for axis, n in (("section", 8), ("tensor", 4), ("dp", 8)):
        me = lax.axis_index(axis)
        for offset in range(1, n):
            place = {"section": comm.z, "tensor": comm.y, "dp": comm.dp}
            place[axis] = lax.rem(me + offset, n)
            peers.append((place["section"], place["tensor"], place["dp"]))
    for peer in peers:
        pl.semaphore_signal(barrier, inc=1, device_id=peer, device_id_type=MESH)

    def weight_copy(i):
        return pltpu.make_async_copy(
            weight_ref.at[pl.ds(pl.multiple_of(i * PAIR, TILE), PAIR)],
            padded.at[pl.ds(pl.multiple_of(i * PADDED, TILE), PAIR)],
            local_sem.at[i],
        )

    for i in range(PAIRS):
        weight_copy(i).start()

    spread = lax.dot_general(
        own_ref[...], selection(odd), (((0,), (0,)), ((), ())), preferred_element_type=F32
    ).astype(BF16)
    low, high = spread[:, :LANES], spread[:, LANES:]
    alone = jnp.where(even, low, high).reshape(7, TILE, LANES)
    shared_out[...] = jnp.where(even, high, low).reshape(7, TILE, LANES)
    pl.semaphore_wait(barrier, len(peers))

    wait = comm.send(shared_out, shared_in, comm.partner())
    for i in range(PAIRS):
        padded[i * PADDED + PAIR : (i + 1) * PADDED] = jnp.zeros((PADDED - PAIR, COLS), BF16)
    logits[...] = jnp.zeros_like(logits)
    wait()
    shared = shared_out[...] + shared_in[...]
    zero_tile = jnp.zeros((1, TILE, LANES), BF16)
    held[comm.z, comm.y, comm.x, comm.c] = jnp.where(
        even,
        jnp.concatenate([alone, shared[0:4]], axis=0),
        jnp.concatenate([shared[4:7], alone, zero_tile], axis=0),
    )

    def add_logits(z, d):
        if d == 0:
            for i in range(PAIRS):
                weight_copy(i).wait()
        logits[...] += jnp.dot(
            load_hidden(held, z),
            padded[pl.ds(pl.multiple_of(z * 2 * PADDED, LANES), 2 * PADDED)],
            preferred_element_type=F32,
        )

    line = comm.line
    gather(comm, held, line, add_logits)

    def column(row):
        return jnp.broadcast_to(row, (LANES, LANES)).T[:, 0:1]

    def target_column(j):
        return column(target_ref[j : j + 1].astype(F32))

    first = ((comm.z * 4 + comm.y) * 8 + comm.dp) * COLS
    columns = first + lax.broadcasted_iota(jnp.int32, (LANES, COLS), 1)
    columns = columns.astype(F32)
    lane = lax.broadcasted_iota(jnp.int32, (LANES, LANES), 1)
    stats[...] = jnp.zeros_like(stats)
    for j in range(TOK // LANES):
        rows = slice(j * LANES, (j + 1) * LANES)
        block = logits[rows]
        top = jnp.max(block, axis=1, keepdims=True)
        total = jnp.sum(jnp.exp(block - top), axis=1, keepdims=True)
        picked = jnp.sum(jnp.where(target_column(j) == columns, block, 0.0), axis=1, keepdims=True)
        turned = jnp.where(lane == 0, top + jnp.log(total), picked).T
        for i in range(2):
            stats[i, j : j + 1] = turned[i : i + 1]

    for axis, n, slots in (("dp", 8, far.at[0]), ("tensor", 4, near), ("section", 8, far.at[1])):
        me = lax.axis_index(axis)
        waits = []
        slots[me] = stats[...]
        for offset in range(1, n):
            place = {"section": comm.z, "tensor": comm.y, "dp": comm.dp}
            place[axis] = lax.rem(me + offset, n)
            waits.append(
                comm.send(
                    slots.at[me],
                    slots.at[me],
                    (place["section"], place["tensor"], place["dp"]),
                    landing=slots.at[lax.rem(me + n - offset, n)],
                )
            )
        for wait in waits:
            wait()
        tops = [slots[i, 0] for i in range(n)]
        top = tops[0]
        for i in range(1, n):
            top = jnp.maximum(top, tops[i])
        total = jnp.exp(tops[0] - top)
        picked = slots[0, 1]
        for i in range(1, n):
            total += jnp.exp(tops[i] - top)
            picked += slots[i, 1]
        stats[0] = top + jnp.log(total)
        stats[1] = picked
        comm.drain()

    log_total = stats[0]
    terms = stats[1] - log_total

    def flat(rows):
        return jnp.concatenate([rows[j : j + 1] for j in range(TOK // LANES)], axis=1)

    token = lax.broadcasted_iota(jnp.int32, (SEQS, TOK), 1)
    start = SEQ * lax.broadcasted_iota(jnp.int32, (SEQS, TOK), 0)
    onehot = jnp.where((token >= start) & (token < start + SEQ), flat(mask_ref[...].astype(F32)), 0.0)
    counts = jnp.sum(onehot, axis=1, keepdims=True)
    seq = (SEQS, SEQS)
    down, right = lax.broadcasted_iota(jnp.int32, seq, 0), lax.broadcasted_iota(jnp.int32, seq, 1)
    pair_down, pair_right = jnp.zeros(seq, jnp.int32), jnp.zeros(seq, jnp.int32)
    ref_down = jnp.zeros(seq, F32)
    for i in range(SEQS):
        pair_down = jnp.where(down == i, pair_ref[i], pair_down)
        pair_right = jnp.where(right == i, pair_ref[i], pair_right)
        ref_down = jnp.where(down == i, ref_ref[i], ref_down)
    same = jnp.where(pair_down == pair_right, 1.0, 0.0)
    earlier = jnp.sum(jnp.where(right < down, same, 0.0), axis=1, keepdims=True)
    sign = jnp.where(earlier == 0.0, 1.0, -1.0)
    eye = down == right

    logprobs = jnp.sum(onehot * flat(terms), axis=1, keepdims=True) / counts
    logprobs_ref[...] = jnp.sum(jnp.where(eye, logprobs, 0.0), axis=0, keepdims=True)
    contrib = sign * (logprobs - ref_down[:, 0:1])
    across = jnp.sum(jnp.where(eye, contrib, 0.0), axis=0, keepdims=True)
    margin = jnp.sum(same * across, axis=1, keepdims=True)
    coefficient = -loss_scale * beta_value * jax.nn.sigmoid(-beta_value * margin) * sign
    token_weight = jnp.sum(onehot * (coefficient / counts), axis=0, keepdims=True)

    for j in range(TOK // LANES):
        rows = slice(j * LANES, (j + 1) * LANES)
        probs = jnp.exp(logits[rows] - column(log_total[j : j + 1]))
        hit = (target_column(j) == columns).astype(F32)
        dlogits[rows] = (column(token_weight[:, rows]) * (hit - probs)).astype(BF16)

    line = comm.line
    ready = {d: Event() for d in FAR_FIRST}

    def hidden_grad(d):
        z = comm.step("z", d)
        for pair in (0, 1):
            terms = lax.dot_general(
                dlogits[...],
                padded[pl.ds(pl.multiple_of((2 * z + pair) * PADDED, LANES), PADDED)],
                (((1,), (1,)), ((), ())),
                preferred_element_type=F32,
            ).astype(BF16)
            left, middle, right = (
                terms[:, i * LANES : (i + 1) * LANES].reshape(4, 2, 7, TILE, LANES) for i in range(3)
            )
            partial[z, 2 * pair, :, :, 0:7] = left
            partial[z, 2 * pair, :, :, 7:11] = middle[:, :, 0:4]
            partial[z, 2 * pair + 1, :, :, 0:3] = middle[:, :, 4:7]
            partial[z, 2 * pair + 1, :, :, 3:10] = right
            partial[z, 2 * pair + 1, :, :, 10:11] = jnp.zeros((4, 2, 1, TILE, LANES), BF16)
        wait = comm.send(partial.at[z, :, :, 1 - comm.c], near_out.at[FAR_FIRST.index(d)], "c", 1)

        def rest():
            yield [wait]
            wait()
            for y in range(4):
                partial[z, y, :, comm.c] = partial[z, y, :, comm.c] + near_out[FAR_FIRST.index(d), y]
            line.busy(ADD_US)
            line.fire(ready[d])

        line.spawn(rest())

    def grad_copy(i):
        return pltpu.make_async_copy(
            padded.at[pl.ds(pl.multiple_of(i * PADDED, TILE), PAIR)],
            weight_grad_ref.at[pl.ds(pl.multiple_of(i * PAIR, TILE), PAIR)],
            local_sem.at[i],
        )

    def weight_grad(z):
        def item():
            block = lax.dot_general(
                load_hidden(held, z), dlogits[...], (((0,), (0,)), ((), ())), preferred_element_type=F32
            )
            padded[z * 2 * PADDED : (z + 1) * 2 * PADDED] = block.astype(BF16)
            grad_copy(2 * z).start()
            grad_copy(2 * z + 1).start()

        return item

    def compute():
        for d in FAR_FIRST:
            hidden_grad(d)
            line.busy(MATMUL_US)
            yield []
        line.work = [weight_grad(z) for z in range(8)]

    line.spawn(compute())
    reduce(comm, partial, final, buffers, line, ready)
    line.run()

    mine = final[...].astype(BF16)
    comm.drain()
    shared_out[0:4] = jnp.where(even, mine[7:11], jnp.concatenate([mine[0:3], mine[0:1]], axis=0))
    comm.send(shared_out.at[0:4], swapped, comm.partner())()
    other = swapped[...]
    alone = jnp.where(even, mine[0:7], mine[3:10]).reshape(ROWS, LANES)
    shared = jnp.where(
        even,
        jnp.concatenate([mine[7:11], other[0:3]], axis=0),
        jnp.concatenate([other, mine[0:3]], axis=0),
    ).reshape(ROWS, LANES)
    both = jnp.concatenate([jnp.where(even, alone, shared), jnp.where(even, shared, alone)], axis=1)
    hidden_grad_ref[...] = lax.dot_general(
        selection(odd), both, (((1,), (1,)), ((), ())), preferred_element_type=F32
    ).astype(BF16)
    comm.drain()
    for i in range(PAIRS):
        grad_copy(i).wait()


def per_device(hidden, head_weight, targets, response_mask, pair_ids, ref_logprobs):
    vmem = pl.BlockSpec(memory_space=pltpu.VMEM)
    smem = pl.BlockSpec(memory_space=pltpu.SMEM)
    hbm = pl.BlockSpec(memory_space=pl.ANY)
    copies = 400
    logprobs, turned, grad_weight = pl.pallas_call(
        kernel,
        out_shape=(
            jax.ShapeDtypeStruct((1, SEQS), F32),
            jax.ShapeDtypeStruct((WIDE, ROWS), BF16),
            jax.ShapeDtypeStruct(head_weight.shape, BF16),
        ),
        in_specs=[smem, smem, vmem, hbm, vmem, vmem],
        out_specs=(vmem, vmem, hbm),
        scratch_shapes=[
            pltpu.VMEM((8, 4, 4, 2, BLOB, TILE, LANES), BF16),
            pltpu.VMEM((8, 4, 4, 2, BLOB, TILE, LANES), BF16),
            pltpu.VMEM((PAIRS * PADDED, COLS), BF16),
            pltpu.VMEM((TOK, COLS), F32),
            pltpu.VMEM((TOK, COLS), BF16),
            pltpu.VMEM((7, TILE, LANES), BF16),
            pltpu.VMEM((7, TILE, LANES), BF16),
            pltpu.VMEM((2, 8, LANES), F32),
            pltpu.VMEM((2, 8, 2, 8, LANES), F32),
            pltpu.VMEM((4, 2, 8, LANES), F32),
            pltpu.VMEM((BLOB, TILE, LANES), F32),
            pltpu.VMEM((8, 4, 4, BLOB, TILE, LANES), BF16),
            pltpu.VMEM((4, TILE, LANES), BF16),
            pltpu.SemaphoreType.DMA((copies,)),
            pltpu.SemaphoreType.DMA((copies,)),
            pltpu.SemaphoreType.DMA((PAIRS,)),
            *reduce_shapes(),
        ],
        compiler_params=pltpu.CompilerParams(
            collective_id=0, has_side_effects=True, vmem_limit_bytes=50 * 1024 * 1024
        ),
        cost_estimate=pl.CostEstimate(
            flops=6 * TOK * 5376 * COLS, bytes_accessed=12 * 1024 * 1024, transcendentals=2 * TOK * COLS
        ),
    )(
        pair_ids, ref_logprobs, hidden.T, head_weight,
        targets.reshape(TOK // LANES, LANES), response_mask.reshape(TOK // LANES, LANES),
    )
    return (logprobs.reshape(SEQS), turned.T, grad_weight)


def solution(mesh):
    placed = (
        P("dp", ("section", "tensor")),
        P(None, ("section", "tensor", "dp")),
        P(),
        P(),
        P(),
        P(),
    )
    return jax.shard_map(
        per_device,
        mesh=mesh,
        in_specs=placed,
        out_specs=(P(), P("dp", ("section", "tensor")), P(None, ("section", "tensor", "dp"))),
        check_vma=False,
    )
```

```python
import heapq
import itertools
import math

import jax
import jax.numpy as jnp
from jax import lax
from jax.experimental import pallas as pl
from jax.experimental.pallas import tpu as pltpu
from jax.sharding import PartitionSpec as P

loss_scale = 2048.0
beta_value = 2.0

MESH = pl.DeviceIdType.MESH
SIZE = {"z": 8, "y": 4, "x": 4}
BLOB = 11
OWN_TILES = 7
CUTS = ((0, 4), (4, 8), (8, 11))
LANES = 128
TILE = 16
ROWS = 112
WIDE = 168
TOK = 896
SEQS = 16
SEQ = 56
COLS = 512
PAIRS = 16
PAIR = 336
PADDED = 384
F32 = jnp.float32
BF16 = jnp.bfloat16
ISSUE_US = 0.02
HOP_US = 1.5
EACH_HOP_US = 0.5
LINK = 45.0e3
CORE_LINK = 600.0e3
MATMUL_US = 0.8
ADD_US = 0.03
FAR_FIRST = (4, 3, -3, 2, -2, 1, -1, 0)


class Comm:
    def __init__(self, send_sem, recv_sem):
        self.z = lax.axis_index("section")
        self.y = lax.axis_index("tensor")
        dp = lax.axis_index("dp")
        self.dp = dp
        self.x = dp // 2
        self.c = lax.rem(dp, 2)
        self.send_sem, self.recv_sem = send_sem, recv_sem
        self.used = 0
        self.unsent = []
        self.line = Timeline()

    def at(self, axis):
        return {"z": self.z, "y": self.y, "x": self.x}[axis]

    def step(self, axis, offset):
        return lax.rem(self.at(axis) + offset + 2 * SIZE[axis], SIZE[axis])

    def device(self, axis, offset):
        z, y, x = self.z, self.y, self.x
        position = self.step(axis, offset)
        if axis == "z":
            z = position
        elif axis == "y":
            y = position
        else:
            x = position
        return (z, y, 2 * x + self.c)

    def sibling(self):
        return (self.z, self.y, 2 * self.x + 1 - self.c)

    def partner(self):
        return (self.z, self.y + 1 - 2 * lax.rem(self.y, 2), self.dp)

    def send(self, src, dst, axis, offset=None, landing=None):
        i = self.used
        self.used += 1
        if offset is None:
            device = axis
        else:
            device = self.sibling() if axis == "c" else self.device(axis, offset)
        copy = pltpu.make_async_remote_copy(
            src_ref=src,
            dst_ref=dst,
            send_sem=self.send_sem.at[i],
            recv_sem=self.recv_sem.at[i],
            device_id=device,
            device_id_type=MESH,
        )
        copy.start()
        self.unsent.append(copy)
        land = dst if landing is None else landing
        back = pltpu.make_async_remote_copy(
            src_ref=land,
            dst_ref=land,
            send_sem=self.send_sem.at[i],
            recv_sem=self.recv_sem.at[i],
            device_id=device,
            device_id_type=MESH,
        )
        size = math.prod(src.shape) * jnp.dtype(src.dtype).itemsize
        when = self.line.now + 2 * HOP_US if offset is None else self.line.carry(axis, offset, size)
        return Landing(self.line, back, when)

    def drain(self):
        for copy in self.unsent:
            copy.wait_send()
        self.unsent = []


class Event:
    def __init__(self):
        self.fired = False
        self.waiting = []


class Landing:
    def __init__(self, line, copy, when):
        self.line, self.copy, self.when = line, copy, when

    def __call__(self):
        self.copy.wait_recv()
        self.line.now = max(self.line.now, self.when)


class Timeline:
    def __init__(self):
        self.now = 0.0
        self.heap = []
        self.order = itertools.count()
        self.work = []
        self.free = {}

    def spawn(self, generator, when=0.0):
        heapq.heappush(self.heap, (max(self.now, when), next(self.order), generator))

    def fire(self, event):
        event.fired = True
        for generator in event.waiting:
            self.spawn(generator)
        event.waiting = []

    def busy(self, us):
        self.now += us

    def carry(self, axis, offset, size):
        self.busy(ISSUE_US)
        link = (axis, offset > 0)
        hops = 1 if axis == "c" else abs(offset)
        us = size / CORE_LINK if axis == "c" else hops * size / LINK
        end = max(self.now, self.free.get(link, 0.0)) + us
        self.free[link] = end
        return end + HOP_US + (EACH_HOP_US * (hops + 1) if axis != "c" else EACH_HOP_US)

    def run(self):
        while self.heap:
            while self.work and self.heap[0][0] > self.now + 0.4 * MATMUL_US:
                self.work.pop(0)()
                self.busy(MATMUL_US)
            when, _, generator = heapq.heappop(self.heap)
            self.now = max(self.now, when)
            while True:
                try:
                    wish = next(generator)
                except StopIteration:
                    break
                if isinstance(wish, Event):
                    if wish.fired:
                        continue
                    wish.waiting.append(generator)
                else:
                    self.spawn(generator, max([landing.when for landing in wish], default=0.0))
                break
        while self.work:
            self.work.pop(0)()
            self.busy(MATMUL_US)


NEAR_FIRST = (1, -1, 2, -2, 3, -3, 4)


def ring_views(comm, array):
    core = comm.c
    (l0, h0), (l1, h1), _ = CUTS

    def cut(lo, hi, half):
        middle = (lo + hi) // 2
        return slice(lo, hi) if half is None else slice(lo, middle) if half == 0 else slice(middle, hi)

    def some(half):
        return slice(None) if half is None else pl.ds(2 * half, 2)

    return (
        (
            ("y", lambda z, y, half=None: array.at[z, y, comm.x, core, cut(l0, h0, half)]),
            ("x", lambda z, x, half=None: array.at[z, some(half), x, core, l0:h0]),
        ),
        (
            ("x", lambda z, x, half=None: array.at[z, comm.y, x, core, cut(l1, h1, half)]),
            ("y", lambda z, y, half=None: array.at[z, y, some(half), core, l1:h1]),
        ),
    )


def third_view(comm, array):
    lo, hi = CUTS[2]

    def view(z, y, half=None):
        return array.at[z, y, slice(None) if half is None else pl.ds(2 * half, 2), comm.c, lo:hi]

    return view


def gather(comm, held, line, add_logits, swap):
    place = (comm.z, comm.y, comm.x, comm.c)
    pieces = {d: [1, 1, 4] for d in FAR_FIRST}
    other = {d: [] for d in FAR_FIRST}

    def finish(part, d):
        pieces[d][part] -= 1
        if pieces[d][part]:
            return
        z = comm.step("z", d)
        cut = slice(*CUTS[part])
        src = held.at[z, :, :, comm.c, cut]
        other[d].append(comm.send(src, src, "c", 1, landing=held.at[z, :, :, 1 - comm.c, cut]))
        if len(other[d]) == 3:
            line.spawn(rest(z, d))

    def rest(z, d):
        yield other[d]
        for wait in other[d]:
            wait()
        add_logits(z, d)
        line.busy(MATMUL_US)

    def ring(axis, view, d):
        z = comm.step("z", d)
        src = view(z, comm.at(axis))
        left = comm.send(src, src, axis, 1, landing=view(z, comm.step(axis, -1)))
        right = comm.send(src, src, axis, -1, landing=view(z, comm.step(axis, 1)))
        yield [left]
        left()
        src = view(z, comm.step(axis, -1), 0)
        left = comm.send(src, src, axis, 1, landing=view(z, comm.step(axis, 2), 0))
        yield [right]
        right()
        src = view(z, comm.step(axis, 1), 1)
        right = comm.send(src, src, axis, -1, landing=view(z, comm.step(axis, 2), 1))
        yield [left, right]
        left()
        right()

    def chain(part, d):
        for axis, view in views[part]:
            yield from ring(axis, view, d)
        finish(part, d)

    views = ring_views(comm, held)
    joined = slice(OWN_TILES, CUTS[1][1])
    first = slice(0, OWN_TILES)
    here = {d: Event() for d in FAR_FIRST}

    def arrive(d, wait):
        yield [wait]
        wait()
        line.spawn(chain(0, d))
        yield here[d]
        line.spawn(chain(1, d))

    def arrive_joined(d, wait):
        yield [wait]
        wait()
        line.fire(here[d])

    def along_z(y):
        third = third_view(comm, held)
        for s in (1, 2, 3, 4):
            h0, h1 = (0, 1) if s == 4 else (None, None)
            src = third(comm.step("z", 1 - s), y, h0)
            left = comm.send(src, src, "z", 1, landing=third(comm.step("z", -s), y, h0))
            src = third(comm.step("z", s - 1), y, h1)
            right = comm.send(src, src, "z", -1, landing=third(comm.step("z", s), y, h1))
            if s == 1:
                finish(2, 0)
            yield [left, right]
            left()
            right()
            if s < 4:
                finish(2, -s)
                finish(2, s)
        finish(2, 4)

    def start_third():
        lo, hi = CUTS[2]
        src = held.at[(*place, slice(lo, hi))]
        waits = [
            comm.send(
                src, src, "x", o, landing=held.at[comm.z, comm.y, comm.step("x", -o), comm.c, lo:hi]
            )
            for o in (1, -1, 2)
        ]
        yield waits
        for wait in waits:
            wait()
        third = third_view(comm, held)
        src = third(comm.z, comm.y)
        waits = [
            comm.send(src, src, "y", o, landing=third(comm.z, comm.step("y", -o))) for o in (1, -1, 2)
        ]
        line.spawn(along_z(comm.y))
        for wait, o in zip(waits, (1, -1, 2)):
            yield [wait]
            wait()
            line.spawn(along_z(comm.step("y", -o)))

    def spread(tiles, then):
        src = held.at[(*place, tiles)]
        for o in NEAR_FIRST:
            landing = held.at[comm.step("z", -o), comm.y, comm.x, comm.c, tiles]
            wait = comm.send(src, src, "z", o, landing=landing)
            line.spawn(then(4 if o == 4 else -o, wait))

    def start():
        yield from swap()
        line.spawn(start_third())
        line.spawn(chain(1, 0))
        spread(joined, arrive_joined)

    line.spawn(start())
    line.spawn(chain(0, 0))

    def begin():
        spread(first, arrive)
        return
        yield

    line.spawn(begin())
    line.run()


def reduce_shapes():
    t0, t1, t2 = (hi - lo for lo, hi in CUTS)
    end = (TILE, LANES)
    shapes = []
    for tiles in (t0, t1):
        shapes += [
            pltpu.VMEM((8, 2, 2, tiles, *end), BF16),
            pltpu.VMEM((8, 2, 4, tiles, *end), BF16),
            pltpu.VMEM((8, 2, tiles // 2, *end), BF16),
            pltpu.VMEM((8, 2, tiles, *end), BF16),
            pltpu.VMEM((7, tiles, *end), BF16),
        ]
    shapes += [
        pltpu.VMEM((4, 2, 2, t2, *end), BF16),
        pltpu.VMEM((4, 3, 2, 4, t2, *end), BF16),
        pltpu.VMEM((3, 4, t2, *end), BF16),
        pltpu.VMEM((4, t2, *end), F32),
        pltpu.VMEM((3, t2, *end), F32),
    ]
    return shapes


def reduce(comm, partial, result, buffers, line, ready, shared_done):
    def add(own, *others):
        if len(others) == 1:
            own[...] = own[...] + others[0][...]
            line.busy(ADD_US)
            return
        total = own[...].astype(F32)
        for other in others:
            total += other[...].astype(F32)
        own[...] = total.astype(own.dtype)
        line.busy(ADD_US)

    def ring(axis, view, d, halves, fulls):
        slot = FAR_FIRST.index(d)
        z = comm.step("z", d)
        left = comm.send(view(z, comm.step(axis, 2), 0), halves.at[slot, 0], axis, 1)
        right = comm.send(view(z, comm.step(axis, 2), 1), halves.at[slot, 1], axis, -1)
        yield [left]
        left()
        add(view(z, comm.step(axis, 1), 0), halves.at[slot, 0])
        left = comm.send(view(z, comm.step(axis, 1)), fulls.at[slot, 0], axis, 1)
        yield [right]
        right()
        add(view(z, comm.step(axis, -1), 1), halves.at[slot, 1])
        right = comm.send(view(z, comm.step(axis, -1)), fulls.at[slot, 1], axis, -1)
        yield [left, right]
        left()
        right()
        add(view(z, comm.at(axis)), fulls.at[slot, 0], fulls.at[slot, 1])

    def side(rings, cut, bufs):
        (near, single), (wide, four) = rings
        landing = bufs[4]
        waits = []
        gate = Event()
        left = [8]

        def chain(d):
            yield ready[d]
            yield from ring(wide, four, d, bufs[0], bufs[1])
            yield from ring(near, single, d, bufs[2], bufs[3])
            if d:
                waits.append(
                    comm.send(single(comm.step("z", d), comm.at(near)), landing.at[len(waits)], "z", d)
                )
            left[0] -= 1
            if left[0] == 0:
                line.fire(gate)

        def rest():
            yield gate
            yield list(waits)
            for wait in waits:
                wait()
            total = single(comm.z, comm.at(near))[...].astype(F32)
            for i in range(7):
                total += landing[i].astype(F32)
            result[cut[0] : cut[1]] = total
            line.busy(ADD_US)
            if cut == CUTS[1]:
                line.fire(shared_done[0])

        for d in FAR_FIRST:
            line.spawn(chain(d))
        line.spawn(rest())

    views = ring_views(comm, partial)
    third = third_view(comm, partial)
    halves, fulls, landing, row, last = buffers[10:15]
    waits = []

    def along_z(slot, o):
        y = comm.step("y", o)
        yield ready[4]
        left = comm.send(third(comm.step("z", 4), y, 0), halves.at[slot, 0], "z", 1)
        right = comm.send(third(comm.step("z", 4), y, 1), halves.at[slot, 1], "z", -1)
        came = (halves.at[slot, 0], halves.at[slot, 1])
        for s in (3, 2, 1):
            yield ready[s]
            yield [left]
            left()
            add(third(comm.step("z", s), y, 0 if s == 3 else None), came[0])
            left = comm.send(third(comm.step("z", s), y), fulls.at[slot, s - 1, 0], "z", 1)
            yield ready[-s]
            yield [right]
            right()
            add(third(comm.step("z", -s), y, 1 if s == 3 else None), came[1])
            right = comm.send(third(comm.step("z", -s), y), fulls.at[slot, s - 1, 1], "z", -1)
            came = (fulls.at[slot, s - 1, 0], fulls.at[slot, s - 1, 1])
        yield ready[0]
        yield [left, right]
        left()
        right()
        mine = third(comm.z, y)
        if o:
            add(mine, *came)
            waits.append(comm.send(mine, landing.at[slot], "y", o))
        else:
            row[...] = mine[...].astype(F32) + came[0][...].astype(F32) + came[1][...].astype(F32)
            line.busy(ADD_US)

    gate = Event()
    pending = [4]

    def one(slot, o):
        yield from along_z(slot, o)
        pending[0] -= 1
        if pending[0] == 0:
            line.fire(gate)

    def rest():
        yield gate
        yield list(waits)
        for wait in waits:
            wait()
        total = row[...]
        for i in range(3):
            total += landing[i].astype(F32)
        row[...] = total
        line.busy(ADD_US)
        ends = [comm.send(row.at[comm.step("x", o)], last.at[k], "x", o) for k, o in enumerate((1, -1, 2))]
        yield ends
        for wait in ends:
            wait()
        result[CUTS[2][0] : CUTS[2][1]] = row[comm.x] + last[0] + last[1] + last[2]
        line.fire(shared_done[1])

    for slot, o in enumerate((2, 1, -1, 0)):
        line.spawn(one(slot, o))
    side(views[0], CUTS[0], buffers[0:5])
    side(views[1], CUTS[1], buffers[5:10])
    line.spawn(rest())


def load_hidden(held, z):
    tiles = []
    for pair in (0, 1):
        even, odd = 2 * pair, 2 * pair + 1
        middle = jnp.concatenate([held[z, even, :, :, 7:11], held[z, odd, :, :, 7:10]], axis=2)
        for part in (held[z, even, :, :, 0:7], middle, held[z, odd, :, :, 0:7]):
            tiles.append(part.reshape(TOK, LANES))
    return jnp.concatenate(tiles, axis=1)


def selection(odd):
    feature = lax.broadcasted_iota(jnp.int32, (WIDE, 2 * LANES), 0)
    place = lax.broadcasted_iota(jnp.int32, (WIDE, 2 * LANES), 1)
    return (place == feature + 40 * odd).astype(F32).astype(BF16)


def kernel(
    pair_ref, ref_ref, own_ref, weight_ref, target_ref, mask_ref,
    logprobs_ref, hidden_grad_ref, weight_grad_ref,
    held, partial, padded, logits, dlogits, shared_out, shared_in, stats, far, near, final, near_out, swapped,
    send_sem, recv_sem, local_sem, *buffers,
):
    comm = Comm(send_sem, recv_sem)
    odd = lax.rem(comm.y, 2)
    even = odd == 0

    barrier = pltpu.get_barrier_semaphore()
    peers = []
    for axis, n in (("section", 8), ("tensor", 4), ("dp", 8)):
        me = lax.axis_index(axis)
        for offset in range(1, n):
            place = {"section": comm.z, "tensor": comm.y, "dp": comm.dp}
            place[axis] = lax.rem(me + offset, n)
            peers.append((place["section"], place["tensor"], place["dp"]))
    for peer in peers:
        pl.semaphore_signal(barrier, inc=1, device_id=peer, device_id_type=MESH)

    def weight_copy(i):
        return pltpu.make_async_copy(
            weight_ref.at[pl.ds(pl.multiple_of(i * PAIR, TILE), PAIR)],
            padded.at[pl.ds(pl.multiple_of(i * PADDED, TILE), PAIR)],
            local_sem.at[i],
        )

    for i in range(PAIRS):
        weight_copy(i).start()

    spread = lax.dot_general(
        own_ref[...], selection(odd), (((0,), (0,)), ((), ())), preferred_element_type=F32
    ).astype(BF16)
    low, high = spread[:, :LANES], spread[:, LANES:]
    alone = jnp.where(even, low, high).reshape(7, TILE, LANES)
    shared_out[...] = jnp.where(even, high, low).reshape(7, TILE, LANES)
    pl.semaphore_wait(barrier, len(peers))

    held[comm.z, comm.y, comm.x, comm.c, 0:OWN_TILES] = alone

    def swap():
        wait = comm.send(shared_out, shared_in, comm.partner())
        for i in range(PAIRS):
            padded[i * PADDED + PAIR : (i + 1) * PADDED] = jnp.zeros((PADDED - PAIR, COLS), BF16)
        logits[...] = jnp.zeros_like(logits)
        yield [wait]
        wait()
        shared = shared_out[...] + shared_in[...]
        held[comm.z, comm.y, comm.x, comm.c, OWN_TILES:BLOB] = jnp.where(
            even,
            shared[0:4],
            jnp.concatenate([shared[4:7], jnp.zeros((1, TILE, LANES), BF16)], axis=0),
        )

    def add_logits(z, d):
        if d == 0:
            for i in range(PAIRS):
                weight_copy(i).wait()
        logits[...] += jnp.dot(
            load_hidden(held, z),
            padded[pl.ds(pl.multiple_of(z * 2 * PADDED, LANES), 2 * PADDED)],
            preferred_element_type=F32,
        )

    line = comm.line
    gather(comm, held, line, add_logits, swap)

    def column(row):
        return jnp.broadcast_to(row, (LANES, LANES)).T[:, 0:1]

    def target_column(j):
        return column(target_ref[j : j + 1].astype(F32))

    first = ((comm.z * 4 + comm.y) * 8 + comm.dp) * COLS
    columns = first + lax.broadcasted_iota(jnp.int32, (LANES, COLS), 1)
    columns = columns.astype(F32)
    lane = lax.broadcasted_iota(jnp.int32, (LANES, LANES), 1)
    stats[...] = jnp.zeros_like(stats)
    for j in range(TOK // LANES):
        rows = slice(j * LANES, (j + 1) * LANES)
        block = logits[rows]
        top = jnp.max(block, axis=1, keepdims=True)
        total = jnp.sum(jnp.exp(block - top), axis=1, keepdims=True)
        picked = jnp.sum(jnp.where(target_column(j) == columns, block, 0.0), axis=1, keepdims=True)
        turned = jnp.where(lane == 0, top + jnp.log(total), picked).T
        for i in range(2):
            stats[i, j : j + 1] = turned[i : i + 1]

    for axis, n, slots in (("dp", 8, far.at[0]), ("tensor", 4, near), ("section", 8, far.at[1])):
        me = lax.axis_index(axis)
        waits = []
        slots[me] = stats[...]
        for offset in range(1, n):
            place = {"section": comm.z, "tensor": comm.y, "dp": comm.dp}
            place[axis] = lax.rem(me + offset, n)
            waits.append(
                comm.send(
                    slots.at[me],
                    slots.at[me],
                    (place["section"], place["tensor"], place["dp"]),
                    landing=slots.at[lax.rem(me + n - offset, n)],
                )
            )
        for wait in waits:
            wait()
        tops = [slots[i, 0] for i in range(n)]
        top = tops[0]
        for i in range(1, n):
            top = jnp.maximum(top, tops[i])
        total = jnp.exp(tops[0] - top)
        picked = slots[0, 1]
        for i in range(1, n):
            total += jnp.exp(tops[i] - top)
            picked += slots[i, 1]
        stats[0] = top + jnp.log(total)
        stats[1] = picked
        comm.drain()

    log_total = stats[0]
    terms = stats[1] - log_total

    def flat(rows):
        return jnp.concatenate([rows[j : j + 1] for j in range(TOK // LANES)], axis=1)

    token = lax.broadcasted_iota(jnp.int32, (SEQS, TOK), 1)
    start = SEQ * lax.broadcasted_iota(jnp.int32, (SEQS, TOK), 0)
    onehot = jnp.where((token >= start) & (token < start + SEQ), flat(mask_ref[...].astype(F32)), 0.0)
    counts = jnp.sum(onehot, axis=1, keepdims=True)
    seq = (SEQS, SEQS)
    down, right = lax.broadcasted_iota(jnp.int32, seq, 0), lax.broadcasted_iota(jnp.int32, seq, 1)
    pair_down, pair_right = jnp.zeros(seq, jnp.int32), jnp.zeros(seq, jnp.int32)
    ref_down = jnp.zeros(seq, F32)
    for i in range(SEQS):
        pair_down = jnp.where(down == i, pair_ref[i], pair_down)
        pair_right = jnp.where(right == i, pair_ref[i], pair_right)
        ref_down = jnp.where(down == i, ref_ref[i], ref_down)
    same = jnp.where(pair_down == pair_right, 1.0, 0.0)
    earlier = jnp.sum(jnp.where(right < down, same, 0.0), axis=1, keepdims=True)
    sign = jnp.where(earlier == 0.0, 1.0, -1.0)
    eye = down == right

    logprobs = jnp.sum(onehot * flat(terms), axis=1, keepdims=True) / counts
    logprobs_ref[...] = jnp.sum(jnp.where(eye, logprobs, 0.0), axis=0, keepdims=True)
    contrib = sign * (logprobs - ref_down[:, 0:1])
    across = jnp.sum(jnp.where(eye, contrib, 0.0), axis=0, keepdims=True)
    margin = jnp.sum(same * across, axis=1, keepdims=True)
    coefficient = -loss_scale * beta_value * jax.nn.sigmoid(-beta_value * margin) * sign
    token_weight = jnp.sum(onehot * (coefficient / counts), axis=0, keepdims=True)

    for j in range(TOK // LANES):
        rows = slice(j * LANES, (j + 1) * LANES)
        probs = jnp.exp(logits[rows] - column(log_total[j : j + 1]))
        hit = (target_column(j) == columns).astype(F32)
        dlogits[rows] = (column(token_weight[:, rows]) * (hit - probs)).astype(BF16)

    line = comm.line
    ready = {d: Event() for d in FAR_FIRST}

    def hidden_grad(d):
        z = comm.step("z", d)
        for pair in (0, 1):
            terms = lax.dot_general(
                dlogits[...],
                padded[pl.ds(pl.multiple_of((2 * z + pair) * PADDED, LANES), PADDED)],
                (((1,), (1,)), ((), ())),
                preferred_element_type=F32,
            ).astype(BF16)
            left, middle, right = (
                terms[:, i * LANES : (i + 1) * LANES].reshape(4, 2, 7, TILE, LANES) for i in range(3)
            )
            partial[z, 2 * pair, :, :, 0:7] = left
            partial[z, 2 * pair, :, :, 7:11] = middle[:, :, 0:4]
            partial[z, 2 * pair + 1, :, :, 0:7] = right
            partial[z, 2 * pair + 1, :, :, 7:10] = middle[:, :, 4:7]
            partial[z, 2 * pair + 1, :, :, 10:11] = jnp.zeros((4, 2, 1, TILE, LANES), BF16)
        wait = comm.send(partial.at[z, :, :, 1 - comm.c], near_out.at[FAR_FIRST.index(d)], "c", 1)

        def rest():
            yield [wait]
            wait()
            for y in range(4):
                partial[z, y, :, comm.c] = partial[z, y, :, comm.c] + near_out[FAR_FIRST.index(d), y]
            line.busy(ADD_US)
            line.fire(ready[d])

        line.spawn(rest())

    def grad_copy(i):
        return pltpu.make_async_copy(
            padded.at[pl.ds(pl.multiple_of(i * PADDED, TILE), PAIR)],
            weight_grad_ref.at[pl.ds(pl.multiple_of(i * PAIR, TILE), PAIR)],
            local_sem.at[i],
        )

    def weight_grad(z):
        def item():
            block = lax.dot_general(
                load_hidden(held, z), dlogits[...], (((0,), (0,)), ((), ())), preferred_element_type=F32
            )
            padded[z * 2 * PADDED : (z + 1) * 2 * PADDED] = block.astype(BF16)
            grad_copy(2 * z).start()
            grad_copy(2 * z + 1).start()

        return item

    def compute():
        for d in FAR_FIRST:
            hidden_grad(d)
            line.busy(MATMUL_US)
            yield []
        line.work = [weight_grad(z) for z in range(8)]

    shared_done = (Event(), Event())

    def swap_back():
        yield shared_done[0]
        yield shared_done[1]
        shared_out[0:4] = final[OWN_TILES:BLOB].astype(BF16)
        wait = comm.send(shared_out.at[0:4], swapped, comm.partner())
        yield [wait]
        wait()

    line.spawn(compute())
    line.spawn(swap_back())
    reduce(comm, partial, final, buffers, line, ready, shared_done)
    line.run()

    mine, other = final[...].astype(BF16), swapped[...]
    alone = mine[0:OWN_TILES].reshape(ROWS, LANES)
    shared = jnp.where(
        even,
        jnp.concatenate([mine[7:11], other[0:3]], axis=0),
        jnp.concatenate([other, mine[7:10]], axis=0),
    ).reshape(ROWS, LANES)
    both = jnp.concatenate([jnp.where(even, alone, shared), jnp.where(even, shared, alone)], axis=1)
    hidden_grad_ref[...] = lax.dot_general(
        selection(odd), both, (((1,), (1,)), ((), ())), preferred_element_type=F32
    ).astype(BF16)
    comm.drain()
    for i in range(PAIRS):
        grad_copy(i).wait()


def move(logprobs_ref, turned_ref, source, logprobs_out, turned_out, result, block, in_sems, out_sems):
    rows = source.shape[0] // PAIRS
    pieces = [pl.ds(i * rows, rows) for i in range(PAIRS)]
    reads = [
        pltpu.make_async_copy(source.at[piece], block.at[piece], in_sems.at[i])
        for i, piece in enumerate(pieces)
    ]
    writes = [
        pltpu.make_async_copy(block.at[piece], result.at[piece], out_sems.at[i])
        for i, piece in enumerate(pieces)
    ]
    for read in reads:
        read.start()
    logprobs_out[...] = logprobs_ref[...]
    turned_out[...] = turned_ref[...]
    for read, write in zip(reads, writes):
        read.wait()
        write.start()
    for write in writes:
        write.wait()


def per_device(hidden, head_weight, targets, response_mask, pair_ids, ref_logprobs):
    vmem = pl.BlockSpec(memory_space=pltpu.VMEM)
    smem = pl.BlockSpec(memory_space=pltpu.SMEM)
    hbm = pl.BlockSpec(memory_space=pl.ANY)
    copies = 448
    logprobs, turned, grad_weight = pl.pallas_call(
        kernel,
        out_shape=(
            jax.ShapeDtypeStruct((1, SEQS), F32),
            jax.ShapeDtypeStruct((WIDE, ROWS), BF16),
            jax.ShapeDtypeStruct(head_weight.shape, BF16),
        ),
        in_specs=[smem, smem, vmem, hbm, vmem, vmem],
        out_specs=(vmem, vmem, hbm),
        scratch_shapes=[
            pltpu.VMEM((8, 4, 4, 2, BLOB, TILE, LANES), BF16),
            pltpu.VMEM((8, 4, 4, 2, BLOB, TILE, LANES), BF16),
            pltpu.VMEM((PAIRS * PADDED, COLS), BF16),
            pltpu.VMEM((TOK, COLS), F32),
            pltpu.VMEM((TOK, COLS), BF16),
            pltpu.VMEM((7, TILE, LANES), BF16),
            pltpu.VMEM((7, TILE, LANES), BF16),
            pltpu.VMEM((2, 8, LANES), F32),
            pltpu.VMEM((2, 8, 2, 8, LANES), F32),
            pltpu.VMEM((4, 2, 8, LANES), F32),
            pltpu.VMEM((BLOB, TILE, LANES), F32),
            pltpu.VMEM((8, 4, 4, BLOB, TILE, LANES), BF16),
            pltpu.VMEM((4, TILE, LANES), BF16),
            pltpu.SemaphoreType.DMA((copies,)),
            pltpu.SemaphoreType.DMA((copies,)),
            pltpu.SemaphoreType.DMA((PAIRS,)),
            *reduce_shapes(),
        ],
        compiler_params=pltpu.CompilerParams(
            collective_id=0, has_side_effects=True, vmem_limit_bytes=60 * 1024 * 1024
        ),
        cost_estimate=pl.CostEstimate(
            flops=6 * TOK * 5376 * COLS, bytes_accessed=12 * 1024 * 1024, transcendentals=2 * TOK * COLS
        ),
    )(
        pair_ids, ref_logprobs, hidden.T, head_weight,
        targets.reshape(TOK // LANES, LANES), response_mask.reshape(TOK // LANES, LANES),
    )
    logprobs, turned, grad_weight = pl.pallas_call(
        move,
        out_shape=(
            jax.ShapeDtypeStruct((1, SEQS), F32),
            jax.ShapeDtypeStruct((WIDE, ROWS), BF16),
            jax.ShapeDtypeStruct(head_weight.shape, BF16),
        ),
        in_specs=[vmem, vmem, hbm],
        out_specs=(vmem, vmem, hbm),
        scratch_shapes=[
            pltpu.VMEM(head_weight.shape, BF16),
            pltpu.SemaphoreType.DMA((PAIRS,)),
            pltpu.SemaphoreType.DMA((PAIRS,)),
        ],
        compiler_params=pltpu.CompilerParams(vmem_limit_bytes=60 * 1024 * 1024),
    )(logprobs, turned, grad_weight)
    return (logprobs.reshape(SEQS), turned.T, grad_weight)


def solution(mesh):
    placed = (
        P("dp", ("section", "tensor")),
        P(None, ("section", "tensor", "dp")),
        P(),
        P(),
        P(),
        P(),
    )
    return jax.shard_map(
        per_device,
        mesh=mesh,
        in_specs=placed,
        out_specs=(P(), P("dp", ("section", "tensor")), P(None, ("section", "tensor", "dp"))),
        check_vma=False,
    )
```

```python
import heapq
import itertools
import math

import jax
import jax.numpy as jnp
from jax import lax
from jax.experimental import pallas as pl
from jax.experimental.pallas import tpu as pltpu
from jax.sharding import PartitionSpec as P

loss_scale = 2048.0
beta_value = 2.0

MESH = pl.DeviceIdType.MESH
SIZE = {"z": 8, "y": 4, "x": 4}
BLOB = 11
OWN_TILES = 7
CUTS = ((0, 4), (4, 8), (8, 11))
LANES = 128
TILE = 16
ROWS = 112
WIDE = 168
TOK = 896
SEQS = 16
SEQ = 56
COLS = 512
PAIRS = 16
PAIR = 336
PADDED = 384
F32 = jnp.float32
BF16 = jnp.bfloat16
ISSUE_US = 0.02
HOP_US = 1.5
EACH_HOP_US = 0.5
LINK = 45.0e3
CORE_LINK = 600.0e3
MATMUL_US = 0.8
ADD_US = 0.03
FAR_FIRST = (4, 3, -3, 2, -2, 1, -1, 0)


class Comm:
    def __init__(self, send_sem, recv_sem):
        self.z = lax.axis_index("section")
        self.y = lax.axis_index("tensor")
        dp = lax.axis_index("dp")
        self.dp = dp
        self.x = dp // 2
        self.c = lax.rem(dp, 2)
        self.send_sem, self.recv_sem = send_sem, recv_sem
        self.used = 0
        self.unsent = []
        self.line = Timeline()

    def at(self, axis):
        return {"z": self.z, "y": self.y, "x": self.x}[axis]

    def step(self, axis, offset):
        return lax.rem(self.at(axis) + offset + 2 * SIZE[axis], SIZE[axis])

    def device(self, axis, offset):
        z, y, x = self.z, self.y, self.x
        position = self.step(axis, offset)
        if axis == "z":
            z = position
        elif axis == "y":
            y = position
        else:
            x = position
        return (z, y, 2 * x + self.c)

    def sibling(self):
        return (self.z, self.y, 2 * self.x + 1 - self.c)

    def partner(self):
        return (self.z, self.y + 1 - 2 * lax.rem(self.y, 2), self.dp)

    def send(self, src, dst, axis, offset=None, landing=None):
        i = self.used
        self.used += 1
        if offset is None:
            device = axis
        else:
            device = self.sibling() if axis == "c" else self.device(axis, offset)
        copy = pltpu.make_async_remote_copy(
            src_ref=src,
            dst_ref=dst,
            send_sem=self.send_sem.at[i],
            recv_sem=self.recv_sem.at[i],
            device_id=device,
            device_id_type=MESH,
        )
        copy.start()
        self.unsent.append(copy)
        land = dst if landing is None else landing
        back = pltpu.make_async_remote_copy(
            src_ref=land,
            dst_ref=land,
            send_sem=self.send_sem.at[i],
            recv_sem=self.recv_sem.at[i],
            device_id=device,
            device_id_type=MESH,
        )
        size = math.prod(src.shape) * jnp.dtype(src.dtype).itemsize
        when = self.line.now + 2 * HOP_US if offset is None else self.line.carry(axis, offset, size)
        return Landing(self.line, back, when)

    def drain(self):
        for copy in self.unsent:
            copy.wait_send()
        self.unsent = []


class Event:
    def __init__(self):
        self.fired = False
        self.waiting = []


class Landing:
    def __init__(self, line, copy, when):
        self.line, self.copy, self.when = line, copy, when

    def __call__(self):
        self.copy.wait_recv()
        self.line.now = max(self.line.now, self.when)


class Timeline:
    def __init__(self):
        self.now = 0.0
        self.heap = []
        self.order = itertools.count()
        self.work = []
        self.free = {}

    def spawn(self, generator, when=0.0):
        heapq.heappush(self.heap, (max(self.now, when), next(self.order), generator))

    def fire(self, event):
        event.fired = True
        for generator in event.waiting:
            self.spawn(generator)
        event.waiting = []

    def busy(self, us):
        self.now += us

    def carry(self, axis, offset, size):
        self.busy(ISSUE_US)
        link = (axis, offset > 0)
        hops = 1 if axis == "c" else abs(offset)
        us = size / CORE_LINK if axis == "c" else hops * size / LINK
        end = max(self.now, self.free.get(link, 0.0)) + us
        self.free[link] = end
        return end + HOP_US + (EACH_HOP_US * (hops + 1) if axis != "c" else EACH_HOP_US)

    def run(self):
        while self.heap:
            while self.work and self.heap[0][0] > self.now + 0.4 * MATMUL_US:
                self.work.pop(0)()
                self.busy(MATMUL_US)
            when, _, generator = heapq.heappop(self.heap)
            self.now = max(self.now, when)
            while True:
                try:
                    wish = next(generator)
                except StopIteration:
                    break
                if isinstance(wish, Event):
                    if wish.fired:
                        continue
                    wish.waiting.append(generator)
                else:
                    self.spawn(generator, max([landing.when for landing in wish], default=0.0))
                break
        while self.work:
            self.work.pop(0)()
            self.busy(MATMUL_US)


SPREAD = (2, -2, 1, -1, 3, -3, 4)


def ring_views(comm, array):
    core = comm.c
    (l0, h0), (l1, h1), _ = CUTS

    def cut(lo, hi, half):
        middle = (lo + hi) // 2
        return slice(lo, hi) if half is None else slice(lo, middle) if half == 0 else slice(middle, hi)

    def some(half):
        return slice(None) if half is None else pl.ds(2 * half, 2)

    return (
        (
            ("y", lambda z, y, half=None: array.at[z, y, comm.x, core, cut(l0, h0, half)]),
            ("x", lambda z, x, half=None: array.at[z, some(half), x, core, l0:h0]),
        ),
        (
            ("x", lambda z, x, half=None: array.at[z, comm.y, x, core, cut(l1, h1, half)]),
            ("y", lambda z, y, half=None: array.at[z, y, some(half), core, l1:h1]),
        ),
    )


def third_view(comm, array):
    lo, hi = CUTS[2]

    def view(z, y, half=None):
        return array.at[z, y, slice(None) if half is None else pl.ds(2 * half, 2), comm.c, lo:hi]

    return view


def gather(comm, held, line, add_logits, swap):
    place = (comm.z, comm.y, comm.x, comm.c)
    pieces = {d: [1, 1, 4] for d in FAR_FIRST}
    other = {d: [] for d in FAR_FIRST}

    def finish(part, d):
        pieces[d][part] -= 1
        if pieces[d][part]:
            return
        z = comm.step("z", d)
        cut = slice(*CUTS[part])
        src = held.at[z, :, :, comm.c, cut]
        other[d].append(comm.send(src, src, "c", 1, landing=held.at[z, :, :, 1 - comm.c, cut]))
        if len(other[d]) == 3:
            line.spawn(rest(z, d))

    def rest(z, d):
        yield other[d]
        for wait in other[d]:
            wait()
        add_logits(z, d)
        line.busy(MATMUL_US)

    def ring(axis, view, d):
        z = comm.step("z", d)
        src = view(z, comm.at(axis))
        left = comm.send(src, src, axis, 1, landing=view(z, comm.step(axis, -1)))
        right = comm.send(src, src, axis, -1, landing=view(z, comm.step(axis, 1)))
        yield [left]
        left()
        src = view(z, comm.step(axis, -1), 0)
        left = comm.send(src, src, axis, 1, landing=view(z, comm.step(axis, 2), 0))
        yield [right]
        right()
        src = view(z, comm.step(axis, 1), 1)
        right = comm.send(src, src, axis, -1, landing=view(z, comm.step(axis, 2), 1))
        yield [left, right]
        left()
        right()

    def chain(part, d):
        for axis, view in views[part]:
            yield from ring(axis, view, d)
        finish(part, d)

    views = ring_views(comm, held)
    joined = slice(OWN_TILES, CUTS[1][1])
    first = slice(0, OWN_TILES)
    here = {d: Event() for d in FAR_FIRST}

    def arrive(d, wait):
        yield [wait]
        wait()
        line.spawn(chain(0, d))
        yield here[d]
        line.spawn(chain(1, d))

    def arrive_joined(d, wait):
        yield [wait]
        wait()
        line.fire(here[d])

    def along_z(y):
        third = third_view(comm, held)
        for s in (1, 2, 3, 4):
            h0, h1 = (0, 1) if s == 4 else (None, None)
            src = third(comm.step("z", 1 - s), y, h0)
            left = comm.send(src, src, "z", 1, landing=third(comm.step("z", -s), y, h0))
            src = third(comm.step("z", s - 1), y, h1)
            right = comm.send(src, src, "z", -1, landing=third(comm.step("z", s), y, h1))
            if s == 1:
                finish(2, 0)
            yield [left, right]
            left()
            right()
            if s < 4:
                finish(2, -s)
                finish(2, s)
        finish(2, 4)

    def start_third():
        lo, hi = CUTS[2]
        src = held.at[(*place, slice(lo, hi))]
        waits = [
            comm.send(
                src, src, "x", o, landing=held.at[comm.z, comm.y, comm.step("x", -o), comm.c, lo:hi]
            )
            for o in (1, -1, 2)
        ]
        yield waits
        for wait in waits:
            wait()
        third = third_view(comm, held)
        src = third(comm.z, comm.y)
        waits = [
            comm.send(src, src, "y", o, landing=third(comm.z, comm.step("y", -o))) for o in (1, -1, 2)
        ]
        line.spawn(along_z(comm.y))
        for wait, o in zip(waits, (1, -1, 2)):
            yield [wait]
            wait()
            line.spawn(along_z(comm.step("y", -o)))

    def spread(tiles, then):
        src = held.at[(*place, tiles)]
        for o in SPREAD:
            landing = held.at[comm.step("z", -o), comm.y, comm.x, comm.c, tiles]
            wait = comm.send(src, src, "z", o, landing=landing)
            line.spawn(then(4 if o == 4 else -o, wait))

    def start():
        yield from swap()
        line.spawn(start_third())
        line.spawn(chain(1, 0))
        spread(joined, arrive_joined)

    line.spawn(start())
    line.spawn(chain(0, 0))

    def begin():
        spread(first, arrive)
        return
        yield

    line.spawn(begin())
    line.run()


def reduce_shapes():
    t0, t1, t2 = (hi - lo for lo, hi in CUTS)
    end = (TILE, LANES)
    shapes = []
    for tiles in (t0, t1):
        shapes += [
            pltpu.VMEM((8, 2, 2, tiles, *end), BF16),
            pltpu.VMEM((8, 2, 4, tiles, *end), BF16),
            pltpu.VMEM((8, 2, tiles // 2, *end), BF16),
            pltpu.VMEM((8, 2, tiles, *end), BF16),
            pltpu.VMEM((7, tiles, *end), BF16),
        ]
    shapes += [
        pltpu.VMEM((4, 2, 2, t2, *end), BF16),
        pltpu.VMEM((4, 3, 2, 4, t2, *end), BF16),
        pltpu.VMEM((3, 4, t2, *end), BF16),
        pltpu.VMEM((4, t2, *end), F32),
        pltpu.VMEM((3, t2, *end), F32),
    ]
    return shapes


def reduce(comm, partial, result, buffers, line, ready, shared_done):
    def add(own, *others):
        if len(others) == 1:
            own[...] = own[...] + others[0][...]
            line.busy(ADD_US)
            return
        total = own[...].astype(F32)
        for other in others:
            total += other[...].astype(F32)
        own[...] = total.astype(own.dtype)
        line.busy(ADD_US)

    def ring(axis, view, d, halves, fulls):
        slot = FAR_FIRST.index(d)
        z = comm.step("z", d)
        left = comm.send(view(z, comm.step(axis, 2), 0), halves.at[slot, 0], axis, 1)
        right = comm.send(view(z, comm.step(axis, 2), 1), halves.at[slot, 1], axis, -1)
        yield [left]
        left()
        add(view(z, comm.step(axis, 1), 0), halves.at[slot, 0])
        left = comm.send(view(z, comm.step(axis, 1)), fulls.at[slot, 0], axis, 1)
        yield [right]
        right()
        add(view(z, comm.step(axis, -1), 1), halves.at[slot, 1])
        right = comm.send(view(z, comm.step(axis, -1)), fulls.at[slot, 1], axis, -1)
        yield [left, right]
        left()
        right()
        add(view(z, comm.at(axis)), fulls.at[slot, 0], fulls.at[slot, 1])

    def side(rings, cut, bufs):
        (near, single), (wide, four) = rings
        landing = bufs[4]
        waits = []
        gate = Event()
        left = [8]

        def chain(d):
            yield ready[d]
            yield from ring(wide, four, d, bufs[0], bufs[1])
            yield from ring(near, single, d, bufs[2], bufs[3])
            if d:
                waits.append(
                    comm.send(single(comm.step("z", d), comm.at(near)), landing.at[len(waits)], "z", d)
                )
            left[0] -= 1
            if left[0] == 0:
                line.fire(gate)

        def rest():
            yield gate
            yield list(waits)
            for wait in waits:
                wait()
            total = single(comm.z, comm.at(near))[...].astype(F32)
            for i in range(7):
                total += landing[i].astype(F32)
            result[cut[0] : cut[1]] = total
            line.busy(ADD_US)
            if cut == CUTS[1]:
                line.fire(shared_done[0])

        for d in FAR_FIRST:
            line.spawn(chain(d))
        line.spawn(rest())

    views = ring_views(comm, partial)
    third = third_view(comm, partial)
    halves, fulls, landing, row, last = buffers[10:15]
    waits = []

    def along_z(slot, o):
        y = comm.step("y", o)
        yield ready[4]
        left = comm.send(third(comm.step("z", 4), y, 0), halves.at[slot, 0], "z", 1)
        right = comm.send(third(comm.step("z", 4), y, 1), halves.at[slot, 1], "z", -1)
        came = (halves.at[slot, 0], halves.at[slot, 1])
        for s in (3, 2, 1):
            yield ready[s]
            yield [left]
            left()
            add(third(comm.step("z", s), y, 0 if s == 3 else None), came[0])
            left = comm.send(third(comm.step("z", s), y), fulls.at[slot, s - 1, 0], "z", 1)
            yield ready[-s]
            yield [right]
            right()
            add(third(comm.step("z", -s), y, 1 if s == 3 else None), came[1])
            right = comm.send(third(comm.step("z", -s), y), fulls.at[slot, s - 1, 1], "z", -1)
            came = (fulls.at[slot, s - 1, 0], fulls.at[slot, s - 1, 1])
        yield ready[0]
        yield [left, right]
        left()
        right()
        mine = third(comm.z, y)
        if o:
            add(mine, *came)
            waits.append(comm.send(mine, landing.at[slot], "y", o))
        else:
            row[...] = mine[...].astype(F32) + came[0][...].astype(F32) + came[1][...].astype(F32)
            line.busy(ADD_US)

    gate = Event()
    pending = [4]

    def one(slot, o):
        yield from along_z(slot, o)
        pending[0] -= 1
        if pending[0] == 0:
            line.fire(gate)

    def rest():
        yield gate
        yield list(waits)
        for wait in waits:
            wait()
        total = row[...]
        for i in range(3):
            total += landing[i].astype(F32)
        row[...] = total
        line.busy(ADD_US)
        ends = [comm.send(row.at[comm.step("x", o)], last.at[k], "x", o) for k, o in enumerate((1, -1, 2))]
        yield ends
        for wait in ends:
            wait()
        result[CUTS[2][0] : CUTS[2][1]] = row[comm.x] + last[0] + last[1] + last[2]
        line.fire(shared_done[1])

    for slot, o in enumerate((2, 1, -1, 0)):
        line.spawn(one(slot, o))
    side(views[0], CUTS[0], buffers[0:5])
    side(views[1], CUTS[1], buffers[5:10])
    line.spawn(rest())


def load_hidden(held, z):
    tiles = []
    for pair in (0, 1):
        even, odd = 2 * pair, 2 * pair + 1
        middle = jnp.concatenate([held[z, even, :, :, 7:11], held[z, odd, :, :, 7:10]], axis=2)
        for part in (held[z, even, :, :, 0:7], middle, held[z, odd, :, :, 0:7]):
            tiles.append(part.reshape(TOK, LANES))
    return jnp.concatenate(tiles, axis=1)


def selection(odd):
    feature = lax.broadcasted_iota(jnp.int32, (WIDE, 2 * LANES), 0)
    place = lax.broadcasted_iota(jnp.int32, (WIDE, 2 * LANES), 1)
    return (place == feature + 40 * odd).astype(F32).astype(BF16)


def kernel(
    pair_ref, ref_ref, own_ref, weight_ref, target_ref, mask_ref,
    logprobs_ref, hidden_grad_ref, weight_grad_ref,
    held, partial, padded, logits, dlogits, shared_out, shared_in, stats, far, near, final, near_out, swapped,
    send_sem, recv_sem, local_sem, *buffers,
):
    comm = Comm(send_sem, recv_sem)
    odd = lax.rem(comm.y, 2)
    even = odd == 0

    barrier = pltpu.get_barrier_semaphore()
    peers = []
    for axis, n in (("section", 8), ("tensor", 4), ("dp", 8)):
        me = lax.axis_index(axis)
        for offset in range(1, n):
            place = {"section": comm.z, "tensor": comm.y, "dp": comm.dp}
            place[axis] = lax.rem(me + offset, n)
            peers.append((place["section"], place["tensor"], place["dp"]))
    for peer in peers:
        pl.semaphore_signal(barrier, inc=1, device_id=peer, device_id_type=MESH)

    def weight_copy(i):
        return pltpu.make_async_copy(
            weight_ref.at[pl.ds(pl.multiple_of(i * PAIR, TILE), PAIR)],
            padded.at[pl.ds(pl.multiple_of(i * PADDED, TILE), PAIR)],
            local_sem.at[i],
        )

    for i in range(PAIRS):
        weight_copy(i).start()

    spread = lax.dot_general(
        own_ref[...], selection(odd), (((0,), (0,)), ((), ())), preferred_element_type=F32
    ).astype(BF16)
    low, high = spread[:, :LANES], spread[:, LANES:]
    alone = jnp.where(even, low, high).reshape(7, TILE, LANES)
    shared_out[...] = jnp.where(even, high, low).reshape(7, TILE, LANES)
    pl.semaphore_wait(barrier, len(peers))

    held[comm.z, comm.y, comm.x, comm.c, 0:OWN_TILES] = alone

    def swap():
        wait = comm.send(shared_out, shared_in, comm.partner())
        for i in range(PAIRS):
            padded[i * PADDED + PAIR : (i + 1) * PADDED] = jnp.zeros((PADDED - PAIR, COLS), BF16)
        logits[...] = jnp.zeros_like(logits)
        yield [wait]
        wait()
        shared = shared_out[...] + shared_in[...]
        held[comm.z, comm.y, comm.x, comm.c, OWN_TILES:BLOB] = jnp.where(
            even,
            shared[0:4],
            jnp.concatenate([shared[4:7], jnp.zeros((1, TILE, LANES), BF16)], axis=0),
        )

    def add_logits(z, d):
        if d == 0:
            for i in range(PAIRS):
                weight_copy(i).wait()
        logits[...] += jnp.dot(
            load_hidden(held, z),
            padded[pl.ds(pl.multiple_of(z * 2 * PADDED, LANES), 2 * PADDED)],
            preferred_element_type=F32,
        )

    line = comm.line
    gather(comm, held, line, add_logits, swap)

    def column(row):
        return jnp.broadcast_to(row, (LANES, LANES)).T[:, 0:1]

    def target_column(j):
        return column(target_ref[j : j + 1].astype(F32))

    first = ((comm.z * 4 + comm.y) * 8 + comm.dp) * COLS
    columns = first + lax.broadcasted_iota(jnp.int32, (LANES, COLS), 1)
    columns = columns.astype(F32)
    lane = lax.broadcasted_iota(jnp.int32, (LANES, LANES), 1)
    stats[...] = jnp.zeros_like(stats)
    for j in range(TOK // LANES):
        rows = slice(j * LANES, (j + 1) * LANES)
        block = logits[rows]
        top = jnp.max(block, axis=1, keepdims=True)
        total = jnp.sum(jnp.exp(block - top), axis=1, keepdims=True)
        picked = jnp.sum(jnp.where(target_column(j) == columns, block, 0.0), axis=1, keepdims=True)
        turned = jnp.where(lane == 0, top + jnp.log(total), picked).T
        for i in range(2):
            stats[i, j : j + 1] = turned[i : i + 1]

    for axis, n, slots in (("dp", 8, far.at[0]), ("tensor", 4, near), ("section", 8, far.at[1])):
        me = lax.axis_index(axis)
        waits = []
        slots[me] = stats[...]
        for offset in range(1, n):
            place = {"section": comm.z, "tensor": comm.y, "dp": comm.dp}
            place[axis] = lax.rem(me + offset, n)
            waits.append(
                comm.send(
                    slots.at[me],
                    slots.at[me],
                    (place["section"], place["tensor"], place["dp"]),
                    landing=slots.at[lax.rem(me + n - offset, n)],
                )
            )
        for wait in waits:
            wait()
        tops = [slots[i, 0] for i in range(n)]
        top = tops[0]
        for i in range(1, n):
            top = jnp.maximum(top, tops[i])
        total = jnp.exp(tops[0] - top)
        picked = slots[0, 1]
        for i in range(1, n):
            total += jnp.exp(tops[i] - top)
            picked += slots[i, 1]
        stats[0] = top + jnp.log(total)
        stats[1] = picked
        comm.drain()

    log_total = stats[0]
    terms = stats[1] - log_total

    def flat(rows):
        return jnp.concatenate([rows[j : j + 1] for j in range(TOK // LANES)], axis=1)

    token = lax.broadcasted_iota(jnp.int32, (SEQS, TOK), 1)
    start = SEQ * lax.broadcasted_iota(jnp.int32, (SEQS, TOK), 0)
    onehot = jnp.where((token >= start) & (token < start + SEQ), flat(mask_ref[...].astype(F32)), 0.0)
    counts = jnp.sum(onehot, axis=1, keepdims=True)
    seq = (SEQS, SEQS)
    down, right = lax.broadcasted_iota(jnp.int32, seq, 0), lax.broadcasted_iota(jnp.int32, seq, 1)
    pair_down, pair_right = jnp.zeros(seq, jnp.int32), jnp.zeros(seq, jnp.int32)
    ref_down = jnp.zeros(seq, F32)
    for i in range(SEQS):
        pair_down = jnp.where(down == i, pair_ref[i], pair_down)
        pair_right = jnp.where(right == i, pair_ref[i], pair_right)
        ref_down = jnp.where(down == i, ref_ref[i], ref_down)
    same = jnp.where(pair_down == pair_right, 1.0, 0.0)
    earlier = jnp.sum(jnp.where(right < down, same, 0.0), axis=1, keepdims=True)
    sign = jnp.where(earlier == 0.0, 1.0, -1.0)
    eye = down == right

    logprobs = jnp.sum(onehot * flat(terms), axis=1, keepdims=True) / counts
    logprobs_ref[...] = jnp.sum(jnp.where(eye, logprobs, 0.0), axis=0, keepdims=True)
    contrib = sign * (logprobs - ref_down[:, 0:1])
    across = jnp.sum(jnp.where(eye, contrib, 0.0), axis=0, keepdims=True)
    margin = jnp.sum(same * across, axis=1, keepdims=True)
    coefficient = -loss_scale * beta_value * jax.nn.sigmoid(-beta_value * margin) * sign
    token_weight = jnp.sum(onehot * (coefficient / counts), axis=0, keepdims=True)

    for j in range(TOK // LANES):
        rows = slice(j * LANES, (j + 1) * LANES)
        probs = jnp.exp(logits[rows] - column(log_total[j : j + 1]))
        hit = (target_column(j) == columns).astype(F32)
        dlogits[rows] = (column(token_weight[:, rows]) * (hit - probs)).astype(BF16)

    line = comm.line
    ready = {d: Event() for d in FAR_FIRST}

    def hidden_grad(d):
        z = comm.step("z", d)
        for pair in (0, 1):
            terms = lax.dot_general(
                dlogits[...],
                padded[pl.ds(pl.multiple_of((2 * z + pair) * PADDED, LANES), PADDED)],
                (((1,), (1,)), ((), ())),
                preferred_element_type=F32,
            ).astype(BF16)
            left, middle, right = (
                terms[:, i * LANES : (i + 1) * LANES].reshape(4, 2, 7, TILE, LANES) for i in range(3)
            )
            partial[z, 2 * pair, :, :, 0:7] = left
            partial[z, 2 * pair, :, :, 7:11] = middle[:, :, 0:4]
            partial[z, 2 * pair + 1, :, :, 0:7] = right
            partial[z, 2 * pair + 1, :, :, 7:10] = middle[:, :, 4:7]
            partial[z, 2 * pair + 1, :, :, 10:11] = jnp.zeros((4, 2, 1, TILE, LANES), BF16)
        wait = comm.send(partial.at[z, :, :, 1 - comm.c], near_out.at[FAR_FIRST.index(d)], "c", 1)

        def rest():
            yield [wait]
            wait()
            for y in range(4):
                partial[z, y, :, comm.c] = partial[z, y, :, comm.c] + near_out[FAR_FIRST.index(d), y]
            line.busy(ADD_US)
            line.fire(ready[d])

        line.spawn(rest())

    def grad_copy(i):
        return pltpu.make_async_copy(
            padded.at[pl.ds(pl.multiple_of(i * PADDED, TILE), PAIR)],
            weight_grad_ref.at[pl.ds(pl.multiple_of(i * PAIR, TILE), PAIR)],
            local_sem.at[i],
        )

    def weight_grad(z):
        def item():
            block = lax.dot_general(
                load_hidden(held, z), dlogits[...], (((0,), (0,)), ((), ())), preferred_element_type=F32
            )
            padded[z * 2 * PADDED : (z + 1) * 2 * PADDED] = block.astype(BF16)
            grad_copy(2 * z).start()
            grad_copy(2 * z + 1).start()

        return item

    def compute():
        for d in FAR_FIRST:
            hidden_grad(d)
            line.busy(MATMUL_US)
            yield []
        line.work = [weight_grad(z) for z in range(8)]

    shared_done = (Event(), Event())

    def swap_back():
        yield shared_done[0]
        yield shared_done[1]
        shared_out[0:4] = final[OWN_TILES:BLOB].astype(BF16)
        wait = comm.send(shared_out.at[0:4], swapped, comm.partner())
        yield [wait]
        wait()

    line.spawn(compute())
    line.spawn(swap_back())
    reduce(comm, partial, final, buffers, line, ready, shared_done)
    line.run()

    mine, other = final[...].astype(BF16), swapped[...]
    alone = mine[0:OWN_TILES].reshape(ROWS, LANES)
    shared = jnp.where(
        even,
        jnp.concatenate([mine[7:11], other[0:3]], axis=0),
        jnp.concatenate([other, mine[7:10]], axis=0),
    ).reshape(ROWS, LANES)
    both = jnp.concatenate([jnp.where(even, alone, shared), jnp.where(even, shared, alone)], axis=1)
    hidden_grad_ref[...] = lax.dot_general(
        selection(odd), both, (((1,), (1,)), ((), ())), preferred_element_type=F32
    ).astype(BF16)
    comm.drain()
    for i in range(PAIRS):
        grad_copy(i).wait()


def move(logprobs_ref, turned_ref, source, logprobs_out, turned_out, result, sems):
    rows = source.shape[0] // PAIRS
    writes = [
        pltpu.make_async_copy(
            source.at[pl.ds(i * rows, rows)], result.at[pl.ds(i * rows, rows)], sems.at[i]
        )
        for i in range(PAIRS)
    ]
    for write in writes:
        write.start()
    logprobs_out[...] = logprobs_ref[...]
    turned_out[...] = turned_ref[...]
    for write in writes:
        write.wait()


def per_device(hidden, head_weight, targets, response_mask, pair_ids, ref_logprobs):
    vmem = pl.BlockSpec(memory_space=pltpu.VMEM)
    smem = pl.BlockSpec(memory_space=pltpu.SMEM)
    hbm = pl.BlockSpec(memory_space=pl.ANY)
    copies = 448
    logprobs, turned, grad_weight = pl.pallas_call(
        kernel,
        out_shape=(
            jax.ShapeDtypeStruct((1, SEQS), F32),
            jax.ShapeDtypeStruct((WIDE, ROWS), BF16),
            jax.ShapeDtypeStruct(head_weight.shape, BF16),
        ),
        in_specs=[smem, smem, vmem, hbm, vmem, vmem],
        out_specs=(vmem, vmem, hbm),
        scratch_shapes=[
            pltpu.VMEM((8, 4, 4, 2, BLOB, TILE, LANES), BF16),
            pltpu.VMEM((8, 4, 4, 2, BLOB, TILE, LANES), BF16),
            pltpu.VMEM((PAIRS * PADDED, COLS), BF16),
            pltpu.VMEM((TOK, COLS), F32),
            pltpu.VMEM((TOK, COLS), BF16),
            pltpu.VMEM((7, TILE, LANES), BF16),
            pltpu.VMEM((7, TILE, LANES), BF16),
            pltpu.VMEM((2, 8, LANES), F32),
            pltpu.VMEM((2, 8, 2, 8, LANES), F32),
            pltpu.VMEM((4, 2, 8, LANES), F32),
            pltpu.VMEM((BLOB, TILE, LANES), F32),
            pltpu.VMEM((8, 4, 4, BLOB, TILE, LANES), BF16),
            pltpu.VMEM((4, TILE, LANES), BF16),
            pltpu.SemaphoreType.DMA((copies,)),
            pltpu.SemaphoreType.DMA((copies,)),
            pltpu.SemaphoreType.DMA((PAIRS,)),
            *reduce_shapes(),
        ],
        compiler_params=pltpu.CompilerParams(
            collective_id=0, has_side_effects=True, vmem_limit_bytes=60 * 1024 * 1024
        ),
        cost_estimate=pl.CostEstimate(
            flops=6 * TOK * 5376 * COLS, bytes_accessed=12 * 1024 * 1024, transcendentals=2 * TOK * COLS
        ),
    )(
        pair_ids, ref_logprobs, hidden.T, head_weight,
        targets.reshape(TOK // LANES, LANES), response_mask.reshape(TOK // LANES, LANES),
    )
    logprobs, turned, grad_weight = pl.pallas_call(
        move,
        out_shape=(
            jax.ShapeDtypeStruct((1, SEQS), F32),
            jax.ShapeDtypeStruct((WIDE, ROWS), BF16),
            jax.ShapeDtypeStruct(head_weight.shape, BF16),
        ),
        in_specs=[vmem, vmem, vmem],
        out_specs=(vmem, vmem, hbm),
        scratch_shapes=[
            pltpu.SemaphoreType.DMA((PAIRS,)),
        ],
        compiler_params=pltpu.CompilerParams(vmem_limit_bytes=16 * 1024 * 1024),
    )(logprobs, turned, grad_weight)
    return (logprobs.reshape(SEQS), turned.T, grad_weight)


def solution(mesh):
    placed = (
        P("dp", ("section", "tensor")),
        P(None, ("section", "tensor", "dp")),
        P(),
        P(),
        P(),
        P(),
    )
    return jax.shard_map(
        per_device,
        mesh=mesh,
        in_specs=placed,
        out_specs=(P(), P("dp", ("section", "tensor")), P(None, ("section", "tensor", "dp"))),
        check_vma=False,
    )
```

```python
import heapq
import itertools
import math

import jax
import jax.numpy as jnp
from jax import lax
from jax.experimental import pallas as pl
from jax.experimental.pallas import tpu as pltpu
from jax.sharding import PartitionSpec as P

loss_scale = 2048.0
beta_value = 2.0

MESH = pl.DeviceIdType.MESH
SIZE = {"z": 8, "y": 4, "x": 4}
BLOB = 11
OWN_TILES = 7
CUTS = ((0, 4), (4, 8), (8, 11))
LANES = 128
TILE = 16
ROWS = 112
WIDE = 168
TOK = 896
SEQS = 16
SEQ = 56
COLS = 512
PAIRS = 16
PAIR = 336
PADDED = 384
F32 = jnp.float32
BF16 = jnp.bfloat16
ISSUE_US = 0.02
HOP_US = 1.5
EACH_HOP_US = 0.5
LINK = 45.0e3
CORE_LINK = 600.0e3
MATMUL_US = 0.8
ADD_US = 0.03
FAR_FIRST = (4, 3, -3, 2, -2, 1, -1, 0)


class Comm:
    def __init__(self, send_sem, recv_sem):
        self.z = lax.axis_index("section")
        self.y = lax.axis_index("tensor")
        dp = lax.axis_index("dp")
        self.dp = dp
        self.x = dp // 2
        self.c = lax.rem(dp, 2)
        self.send_sem, self.recv_sem = send_sem, recv_sem
        self.used = 0
        self.unsent = []
        self.line = Timeline()

    def at(self, axis):
        return {"z": self.z, "y": self.y, "x": self.x}[axis]

    def step(self, axis, offset):
        return lax.rem(self.at(axis) + offset + 2 * SIZE[axis], SIZE[axis])

    def device(self, axis, offset):
        z, y, x = self.z, self.y, self.x
        position = self.step(axis, offset)
        if axis == "z":
            z = position
        elif axis == "y":
            y = position
        else:
            x = position
        return (z, y, 2 * x + self.c)

    def sibling(self):
        return (self.z, self.y, 2 * self.x + 1 - self.c)

    def partner(self):
        return (self.z, self.y + 1 - 2 * lax.rem(self.y, 2), self.dp)

    def send(self, src, dst, axis, offset=None, landing=None):
        i = self.used
        self.used += 1
        if offset is None:
            device = axis
        else:
            device = self.sibling() if axis == "c" else self.device(axis, offset)
        copy = pltpu.make_async_remote_copy(
            src_ref=src,
            dst_ref=dst,
            send_sem=self.send_sem.at[i],
            recv_sem=self.recv_sem.at[i],
            device_id=device,
            device_id_type=MESH,
        )
        copy.start()
        self.unsent.append(copy)
        land = dst if landing is None else landing
        back = pltpu.make_async_remote_copy(
            src_ref=land,
            dst_ref=land,
            send_sem=self.send_sem.at[i],
            recv_sem=self.recv_sem.at[i],
            device_id=device,
            device_id_type=MESH,
        )
        size = math.prod(src.shape) * jnp.dtype(src.dtype).itemsize
        when = self.line.now + 2 * HOP_US if offset is None else self.line.carry(axis, offset, size)
        return Landing(self.line, back, when)

    def drain(self):
        for copy in self.unsent:
            copy.wait_send()
        self.unsent = []


class Event:
    def __init__(self):
        self.fired = False
        self.waiting = []


class Landing:
    def __init__(self, line, copy, when):
        self.line, self.copy, self.when = line, copy, when

    def __call__(self):
        self.copy.wait_recv()
        self.line.now = max(self.line.now, self.when)


class Timeline:
    def __init__(self):
        self.now = 0.0
        self.heap = []
        self.order = itertools.count()
        self.work = []
        self.free = {}

    def spawn(self, generator, when=0.0):
        heapq.heappush(self.heap, (max(self.now, when), next(self.order), generator))

    def fire(self, event):
        event.fired = True
        for generator in event.waiting:
            self.spawn(generator)
        event.waiting = []

    def busy(self, us):
        self.now += us

    def carry(self, axis, offset, size):
        self.busy(ISSUE_US)
        link = (axis, offset > 0)
        hops = 1 if axis == "c" else abs(offset)
        us = size / CORE_LINK if axis == "c" else hops * size / LINK
        end = max(self.now, self.free.get(link, 0.0)) + us
        self.free[link] = end
        return end + HOP_US + (EACH_HOP_US * (hops + 1) if axis != "c" else EACH_HOP_US)

    def run(self):
        while self.heap:
            while self.work and self.heap[0][0] > self.now + 0.4 * MATMUL_US:
                self.work.pop(0)()
                self.busy(MATMUL_US)
            when, _, generator = heapq.heappop(self.heap)
            self.now = max(self.now, when)
            while True:
                try:
                    wish = next(generator)
                except StopIteration:
                    break
                if isinstance(wish, Event):
                    if wish.fired:
                        continue
                    wish.waiting.append(generator)
                else:
                    self.spawn(generator, max([landing.when for landing in wish], default=0.0))
                break
        while self.work:
            self.work.pop(0)()
            self.busy(MATMUL_US)


SPREAD = (2, -2, 1, -1, 3, -3, 4)
GATHER_AT_ONCE = (0,)


def ring_views(comm, array):
    core = comm.c
    (l0, h0), (l1, h1), _ = CUTS

    def cut(lo, hi, half):
        middle = (lo + hi) // 2
        return slice(lo, hi) if half is None else slice(lo, middle) if half == 0 else slice(middle, hi)

    def some(half):
        return slice(None) if half is None else pl.ds(2 * half, 2)

    return (
        (
            ("y", lambda z, y, half=None: array.at[z, y, comm.x, core, cut(l0, h0, half)]),
            ("x", lambda z, x, half=None: array.at[z, some(half), x, core, l0:h0]),
        ),
        (
            ("x", lambda z, x, half=None: array.at[z, comm.y, x, core, cut(l1, h1, half)]),
            ("y", lambda z, y, half=None: array.at[z, y, some(half), core, l1:h1]),
        ),
    )


def third_view(comm, array):
    lo, hi = CUTS[2]

    def view(z, y, half=None):
        return array.at[z, y, slice(None) if half is None else pl.ds(2 * half, 2), comm.c, lo:hi]

    return view


def gather(comm, held, line, add_logits, swap):
    place = (comm.z, comm.y, comm.x, comm.c)
    pieces = {d: [1, 1, 4] for d in FAR_FIRST}
    other = {d: [] for d in FAR_FIRST}

    def finish(part, d):
        pieces[d][part] -= 1
        if pieces[d][part]:
            return
        z = comm.step("z", d)
        cut = slice(*CUTS[part])
        src = held.at[z, :, :, comm.c, cut]
        other[d].append(comm.send(src, src, "c", 1, landing=held.at[z, :, :, 1 - comm.c, cut]))
        if len(other[d]) == 3:
            line.spawn(rest(z, d))

    def rest(z, d):
        yield other[d]
        for wait in other[d]:
            wait()
        add_logits(z, d)
        line.busy(MATMUL_US)

    def ring(axis, view, d):
        z = comm.step("z", d)
        src = view(z, comm.at(axis))
        left = comm.send(src, src, axis, 1, landing=view(z, comm.step(axis, -1)))
        right = comm.send(src, src, axis, -1, landing=view(z, comm.step(axis, 1)))
        yield [left]
        left()
        src = view(z, comm.step(axis, -1), 0)
        left = comm.send(src, src, axis, 1, landing=view(z, comm.step(axis, 2), 0))
        yield [right]
        right()
        src = view(z, comm.step(axis, 1), 1)
        right = comm.send(src, src, axis, -1, landing=view(z, comm.step(axis, 2), 1))
        yield [left, right]
        left()
        right()

    def at_once(axis, view, d):
        z = comm.step("z", d)
        src = view(z, comm.at(axis))
        waits = [
            comm.send(src, src, axis, o, landing=view(z, comm.step(axis, -o))) for o in (1, -1, 2)
        ]
        yield waits
        for wait in waits:
            wait()

    def chain(part, d):
        near, far = views[part]
        yield from (at_once if d in GATHER_AT_ONCE else ring)(*near, d)
        yield from ring(*far, d)
        finish(part, d)

    views = ring_views(comm, held)
    joined = slice(OWN_TILES, CUTS[1][1])
    first = slice(0, OWN_TILES)
    here = {d: Event() for d in FAR_FIRST}

    def arrive(d, wait):
        yield [wait]
        wait()
        line.spawn(chain(0, d))
        yield here[d]
        line.spawn(chain(1, d))

    def arrive_joined(d, wait):
        yield [wait]
        wait()
        line.fire(here[d])

    def along_z(y):
        third = third_view(comm, held)
        for s in (1, 2, 3, 4):
            h0, h1 = (0, 1) if s == 4 else (None, None)
            src = third(comm.step("z", 1 - s), y, h0)
            left = comm.send(src, src, "z", 1, landing=third(comm.step("z", -s), y, h0))
            src = third(comm.step("z", s - 1), y, h1)
            right = comm.send(src, src, "z", -1, landing=third(comm.step("z", s), y, h1))
            if s == 1:
                finish(2, 0)
            yield [left, right]
            left()
            right()
            if s < 4:
                finish(2, -s)
                finish(2, s)
        finish(2, 4)

    def start_third():
        lo, hi = CUTS[2]
        src = held.at[(*place, slice(lo, hi))]
        waits = [
            comm.send(
                src, src, "x", o, landing=held.at[comm.z, comm.y, comm.step("x", -o), comm.c, lo:hi]
            )
            for o in (1, -1, 2)
        ]
        yield waits
        for wait in waits:
            wait()
        third = third_view(comm, held)
        src = third(comm.z, comm.y)
        waits = [
            comm.send(src, src, "y", o, landing=third(comm.z, comm.step("y", -o))) for o in (1, -1, 2)
        ]
        line.spawn(along_z(comm.y))
        for wait, o in zip(waits, (1, -1, 2)):
            yield [wait]
            wait()
            line.spawn(along_z(comm.step("y", -o)))

    def spread(tiles, then):
        src = held.at[(*place, tiles)]
        for o in SPREAD:
            landing = held.at[comm.step("z", -o), comm.y, comm.x, comm.c, tiles]
            wait = comm.send(src, src, "z", o, landing=landing)
            line.spawn(then(4 if o == 4 else -o, wait))

    def start():
        yield from swap()
        line.spawn(start_third())
        line.spawn(chain(1, 0))
        spread(joined, arrive_joined)

    line.spawn(start())
    line.spawn(chain(0, 0))

    def begin():
        spread(first, arrive)
        return
        yield

    line.spawn(begin())
    line.run()


def reduce_shapes():
    t0, t1, t2 = (hi - lo for lo, hi in CUTS)
    end = (TILE, LANES)
    shapes = []
    for tiles in (t0, t1):
        shapes += [
            pltpu.VMEM((8, 2, 2, tiles, *end), BF16),
            pltpu.VMEM((8, 2, 4, tiles, *end), BF16),
            pltpu.VMEM((8, 2, tiles // 2, *end), BF16),
            pltpu.VMEM((8, 2, tiles, *end), BF16),
            pltpu.VMEM((7, tiles, *end), BF16),
        ]
    shapes += [
        pltpu.VMEM((4, 2, 2, t2, *end), BF16),
        pltpu.VMEM((4, 3, 2, 4, t2, *end), BF16),
        pltpu.VMEM((3, 4, t2, *end), BF16),
        pltpu.VMEM((4, t2, *end), F32),
        pltpu.VMEM((3, t2, *end), F32),
    ]
    return shapes


def reduce(comm, partial, result, buffers, line, ready, shared_done):
    def add(own, *others):
        if len(others) == 1:
            own[...] = own[...] + others[0][...]
            line.busy(ADD_US)
            return
        total = own[...].astype(F32)
        for other in others:
            total += other[...].astype(F32)
        own[...] = total.astype(own.dtype)
        line.busy(ADD_US)

    def ring(axis, view, d, halves, fulls):
        slot = FAR_FIRST.index(d)
        z = comm.step("z", d)
        left = comm.send(view(z, comm.step(axis, 2), 0), halves.at[slot, 0], axis, 1)
        right = comm.send(view(z, comm.step(axis, 2), 1), halves.at[slot, 1], axis, -1)
        yield [left]
        left()
        add(view(z, comm.step(axis, 1), 0), halves.at[slot, 0])
        left = comm.send(view(z, comm.step(axis, 1)), fulls.at[slot, 0], axis, 1)
        yield [right]
        right()
        add(view(z, comm.step(axis, -1), 1), halves.at[slot, 1])
        right = comm.send(view(z, comm.step(axis, -1)), fulls.at[slot, 1], axis, -1)
        yield [left, right]
        left()
        right()
        add(view(z, comm.at(axis)), fulls.at[slot, 0], fulls.at[slot, 1])

    def side(rings, cut, bufs):
        (near, single), (wide, four) = rings
        landing = bufs[4]
        waits = []
        gate = Event()
        left = [8]

        def chain(d):
            yield ready[d]
            yield from ring(wide, four, d, bufs[0], bufs[1])
            yield from ring(near, single, d, bufs[2], bufs[3])
            if d:
                waits.append(
                    comm.send(single(comm.step("z", d), comm.at(near)), landing.at[len(waits)], "z", d)
                )
            left[0] -= 1
            if left[0] == 0:
                line.fire(gate)

        def rest():
            yield gate
            yield list(waits)
            for wait in waits:
                wait()
            total = single(comm.z, comm.at(near))[...].astype(F32)
            for i in range(7):
                total += landing[i].astype(F32)
            result[cut[0] : cut[1]] = total
            line.busy(ADD_US)
            if cut == CUTS[1]:
                line.fire(shared_done[0])

        for d in FAR_FIRST:
            line.spawn(chain(d))
        line.spawn(rest())

    views = ring_views(comm, partial)
    third = third_view(comm, partial)
    halves, fulls, landing, row, last = buffers[10:15]
    waits = []

    def along_z(slot, o):
        y = comm.step("y", o)
        yield ready[4]
        left = comm.send(third(comm.step("z", 4), y, 0), halves.at[slot, 0], "z", 1)
        right = comm.send(third(comm.step("z", 4), y, 1), halves.at[slot, 1], "z", -1)
        came = (halves.at[slot, 0], halves.at[slot, 1])
        for s in (3, 2, 1):
            yield ready[s]
            yield [left]
            left()
            add(third(comm.step("z", s), y, 0 if s == 3 else None), came[0])
            left = comm.send(third(comm.step("z", s), y), fulls.at[slot, s - 1, 0], "z", 1)
            yield ready[-s]
            yield [right]
            right()
            add(third(comm.step("z", -s), y, 1 if s == 3 else None), came[1])
            right = comm.send(third(comm.step("z", -s), y), fulls.at[slot, s - 1, 1], "z", -1)
            came = (fulls.at[slot, s - 1, 0], fulls.at[slot, s - 1, 1])
        yield ready[0]
        yield [left, right]
        left()
        right()
        mine = third(comm.z, y)
        if o:
            add(mine, *came)
            waits.append(comm.send(mine, landing.at[slot], "y", o))
        else:
            row[...] = mine[...].astype(F32) + came[0][...].astype(F32) + came[1][...].astype(F32)
            line.busy(ADD_US)

    gate = Event()
    pending = [4]

    def one(slot, o):
        yield from along_z(slot, o)
        pending[0] -= 1
        if pending[0] == 0:
            line.fire(gate)

    def rest():
        yield gate
        yield list(waits)
        for wait in waits:
            wait()
        total = row[...]
        for i in range(3):
            total += landing[i].astype(F32)
        row[...] = total
        line.busy(ADD_US)
        ends = [comm.send(row.at[comm.step("x", o)], last.at[k], "x", o) for k, o in enumerate((1, -1, 2))]
        yield ends
        for wait in ends:
            wait()
        result[CUTS[2][0] : CUTS[2][1]] = row[comm.x] + last[0] + last[1] + last[2]
        line.fire(shared_done[1])

    for slot, o in enumerate((2, 1, -1, 0)):
        line.spawn(one(slot, o))
    side(views[0], CUTS[0], buffers[0:5])
    side(views[1], CUTS[1], buffers[5:10])
    line.spawn(rest())


def load_hidden(held, z):
    tiles = []
    for pair in (0, 1):
        even, odd = 2 * pair, 2 * pair + 1
        middle = jnp.concatenate([held[z, even, :, :, 7:11], held[z, odd, :, :, 7:10]], axis=2)
        for part in (held[z, even, :, :, 0:7], middle, held[z, odd, :, :, 0:7]):
            tiles.append(part.reshape(TOK, LANES))
    return jnp.concatenate(tiles, axis=1)


def selection(odd):
    feature = lax.broadcasted_iota(jnp.int32, (WIDE, 2 * LANES), 0)
    place = lax.broadcasted_iota(jnp.int32, (WIDE, 2 * LANES), 1)
    return (place == feature + 40 * odd).astype(F32).astype(BF16)


def kernel(
    pair_ref, ref_ref, own_ref, weight_ref, target_ref, mask_ref,
    logprobs_ref, hidden_grad_ref, weight_grad_ref,
    held, partial, padded, logits, dlogits, shared_out, shared_in, stats, far, near, final, near_out, swapped,
    send_sem, recv_sem, local_sem, *buffers,
):
    comm = Comm(send_sem, recv_sem)
    odd = lax.rem(comm.y, 2)
    even = odd == 0

    barrier = pltpu.get_barrier_semaphore()
    peers = []
    for axis, n in (("section", 8), ("tensor", 4), ("dp", 8)):
        me = lax.axis_index(axis)
        for offset in range(1, n):
            place = {"section": comm.z, "tensor": comm.y, "dp": comm.dp}
            place[axis] = lax.rem(me + offset, n)
            peers.append((place["section"], place["tensor"], place["dp"]))
    for peer in peers:
        pl.semaphore_signal(barrier, inc=1, device_id=peer, device_id_type=MESH)

    def weight_copy(i):
        return pltpu.make_async_copy(
            weight_ref.at[pl.ds(pl.multiple_of(i * PAIR, TILE), PAIR)],
            padded.at[pl.ds(pl.multiple_of(i * PADDED, TILE), PAIR)],
            local_sem.at[i],
        )

    for i in range(PAIRS):
        weight_copy(i).start()

    spread = lax.dot_general(
        own_ref[...], selection(odd), (((0,), (0,)), ((), ())), preferred_element_type=F32
    ).astype(BF16)
    low, high = spread[:, :LANES], spread[:, LANES:]
    alone = jnp.where(even, low, high).reshape(7, TILE, LANES)
    shared_out[...] = jnp.where(even, high, low).reshape(7, TILE, LANES)
    pl.semaphore_wait(barrier, len(peers))

    held[comm.z, comm.y, comm.x, comm.c, 0:OWN_TILES] = alone

    def swap():
        wait = comm.send(shared_out, shared_in, comm.partner())
        for i in range(PAIRS):
            padded[i * PADDED + PAIR : (i + 1) * PADDED] = jnp.zeros((PADDED - PAIR, COLS), BF16)
        logits[...] = jnp.zeros_like(logits)
        yield [wait]
        wait()
        shared = shared_out[...] + shared_in[...]
        held[comm.z, comm.y, comm.x, comm.c, OWN_TILES:BLOB] = jnp.where(
            even,
            shared[0:4],
            jnp.concatenate([shared[4:7], jnp.zeros((1, TILE, LANES), BF16)], axis=0),
        )

    def add_logits(z, d):
        if d == 0:
            for i in range(PAIRS):
                weight_copy(i).wait()
        logits[...] += jnp.dot(
            load_hidden(held, z),
            padded[pl.ds(pl.multiple_of(z * 2 * PADDED, LANES), 2 * PADDED)],
            preferred_element_type=F32,
        )

    line = comm.line
    gather(comm, held, line, add_logits, swap)

    def column(row):
        return jnp.broadcast_to(row, (LANES, LANES)).T[:, 0:1]

    def target_column(j):
        return column(target_ref[j : j + 1].astype(F32))

    first = ((comm.z * 4 + comm.y) * 8 + comm.dp) * COLS
    columns = first + lax.broadcasted_iota(jnp.int32, (LANES, COLS), 1)
    columns = columns.astype(F32)
    lane = lax.broadcasted_iota(jnp.int32, (LANES, LANES), 1)
    stats[...] = jnp.zeros_like(stats)
    for j in range(TOK // LANES):
        rows = slice(j * LANES, (j + 1) * LANES)
        block = logits[rows]
        top = jnp.max(block, axis=1, keepdims=True)
        total = jnp.sum(jnp.exp(block - top), axis=1, keepdims=True)
        picked = jnp.sum(jnp.where(target_column(j) == columns, block, 0.0), axis=1, keepdims=True)
        turned = jnp.where(lane == 0, top + jnp.log(total), picked).T
        for i in range(2):
            stats[i, j : j + 1] = turned[i : i + 1]

    for axis, n, slots in (("dp", 8, far.at[0]), ("tensor", 4, near), ("section", 8, far.at[1])):
        me = lax.axis_index(axis)
        waits = []
        slots[me] = stats[...]
        for offset in range(1, n):
            place = {"section": comm.z, "tensor": comm.y, "dp": comm.dp}
            place[axis] = lax.rem(me + offset, n)
            waits.append(
                comm.send(
                    slots.at[me],
                    slots.at[me],
                    (place["section"], place["tensor"], place["dp"]),
                    landing=slots.at[lax.rem(me + n - offset, n)],
                )
            )
        for wait in waits:
            wait()
        tops = [slots[i, 0] for i in range(n)]
        top = tops[0]
        for i in range(1, n):
            top = jnp.maximum(top, tops[i])
        total = jnp.exp(tops[0] - top)
        picked = slots[0, 1]
        for i in range(1, n):
            total += jnp.exp(tops[i] - top)
            picked += slots[i, 1]
        stats[0] = top + jnp.log(total)
        stats[1] = picked
        comm.drain()

    log_total = stats[0]
    terms = stats[1] - log_total

    def flat(rows):
        return jnp.concatenate([rows[j : j + 1] for j in range(TOK // LANES)], axis=1)

    token = lax.broadcasted_iota(jnp.int32, (SEQS, TOK), 1)
    start = SEQ * lax.broadcasted_iota(jnp.int32, (SEQS, TOK), 0)
    onehot = jnp.where((token >= start) & (token < start + SEQ), flat(mask_ref[...].astype(F32)), 0.0)
    counts = jnp.sum(onehot, axis=1, keepdims=True)
    seq = (SEQS, SEQS)
    down, right = lax.broadcasted_iota(jnp.int32, seq, 0), lax.broadcasted_iota(jnp.int32, seq, 1)
    pair_down, pair_right = jnp.zeros(seq, jnp.int32), jnp.zeros(seq, jnp.int32)
    ref_down = jnp.zeros(seq, F32)
    for i in range(SEQS):
        pair_down = jnp.where(down == i, pair_ref[i], pair_down)
        pair_right = jnp.where(right == i, pair_ref[i], pair_right)
        ref_down = jnp.where(down == i, ref_ref[i], ref_down)
    same = jnp.where(pair_down == pair_right, 1.0, 0.0)
    earlier = jnp.sum(jnp.where(right < down, same, 0.0), axis=1, keepdims=True)
    sign = jnp.where(earlier == 0.0, 1.0, -1.0)
    eye = down == right

    logprobs = jnp.sum(onehot * flat(terms), axis=1, keepdims=True) / counts
    logprobs_ref[...] = jnp.sum(jnp.where(eye, logprobs, 0.0), axis=0, keepdims=True)
    contrib = sign * (logprobs - ref_down[:, 0:1])
    across = jnp.sum(jnp.where(eye, contrib, 0.0), axis=0, keepdims=True)
    margin = jnp.sum(same * across, axis=1, keepdims=True)
    coefficient = -loss_scale * beta_value * jax.nn.sigmoid(-beta_value * margin) * sign
    token_weight = jnp.sum(onehot * (coefficient / counts), axis=0, keepdims=True)

    for j in range(TOK // LANES):
        rows = slice(j * LANES, (j + 1) * LANES)
        probs = jnp.exp(logits[rows] - column(log_total[j : j + 1]))
        hit = (target_column(j) == columns).astype(F32)
        dlogits[rows] = (column(token_weight[:, rows]) * (hit - probs)).astype(BF16)

    line = comm.line
    ready = {d: Event() for d in FAR_FIRST}

    def hidden_grad(d):
        z = comm.step("z", d)
        for pair in (0, 1):
            terms = lax.dot_general(
                dlogits[...],
                padded[pl.ds(pl.multiple_of((2 * z + pair) * PADDED, LANES), PADDED)],
                (((1,), (1,)), ((), ())),
                preferred_element_type=F32,
            ).astype(BF16)
            left, middle, right = (
                terms[:, i * LANES : (i + 1) * LANES].reshape(4, 2, 7, TILE, LANES) for i in range(3)
            )
            partial[z, 2 * pair, :, :, 0:7] = left
            partial[z, 2 * pair, :, :, 7:11] = middle[:, :, 0:4]
            partial[z, 2 * pair + 1, :, :, 0:7] = right
            partial[z, 2 * pair + 1, :, :, 7:10] = middle[:, :, 4:7]
            partial[z, 2 * pair + 1, :, :, 10:11] = jnp.zeros((4, 2, 1, TILE, LANES), BF16)
        wait = comm.send(partial.at[z, :, :, 1 - comm.c], near_out.at[FAR_FIRST.index(d)], "c", 1)

        def rest():
            yield [wait]
            wait()
            for y in range(4):
                partial[z, y, :, comm.c] = partial[z, y, :, comm.c] + near_out[FAR_FIRST.index(d), y]
            line.busy(ADD_US)
            line.fire(ready[d])

        line.spawn(rest())

    def grad_copy(i):
        return pltpu.make_async_copy(
            padded.at[pl.ds(pl.multiple_of(i * PADDED, TILE), PAIR)],
            weight_grad_ref.at[pl.ds(pl.multiple_of(i * PAIR, TILE), PAIR)],
            local_sem.at[i],
        )

    def weight_grad(z):
        def item():
            block = lax.dot_general(
                load_hidden(held, z), dlogits[...], (((0,), (0,)), ((), ())), preferred_element_type=F32
            )
            padded[z * 2 * PADDED : (z + 1) * 2 * PADDED] = block.astype(BF16)
            grad_copy(2 * z).start()
            grad_copy(2 * z + 1).start()

        return item

    def compute():
        for d in FAR_FIRST:
            hidden_grad(d)
            line.busy(MATMUL_US)
            yield []
        line.work = [weight_grad(z) for z in range(8)]

    shared_done = (Event(), Event())

    def swap_back():
        yield shared_done[0]
        yield shared_done[1]
        shared_out[0:4] = final[OWN_TILES:BLOB].astype(BF16)
        wait = comm.send(shared_out.at[0:4], swapped, comm.partner())
        yield [wait]
        wait()

    line.spawn(compute())
    line.spawn(swap_back())
    reduce(comm, partial, final, buffers, line, ready, shared_done)
    line.run()

    mine, other = final[...].astype(BF16), swapped[...]
    alone = mine[0:OWN_TILES].reshape(ROWS, LANES)
    shared = jnp.where(
        even,
        jnp.concatenate([mine[7:11], other[0:3]], axis=0),
        jnp.concatenate([other, mine[7:10]], axis=0),
    ).reshape(ROWS, LANES)
    both = jnp.concatenate([jnp.where(even, alone, shared), jnp.where(even, shared, alone)], axis=1)
    hidden_grad_ref[...] = lax.dot_general(
        selection(odd), both, (((1,), (1,)), ((), ())), preferred_element_type=F32
    ).astype(BF16)
    comm.drain()
    for i in range(PAIRS):
        grad_copy(i).wait()


def move(logprobs_ref, turned_ref, source, logprobs_out, turned_out, result, sems):
    rows = source.shape[0] // PAIRS
    writes = [
        pltpu.make_async_copy(
            source.at[pl.ds(i * rows, rows)], result.at[pl.ds(i * rows, rows)], sems.at[i]
        )
        for i in range(PAIRS)
    ]
    for write in writes:
        write.start()
    logprobs_out[...] = logprobs_ref[...]
    turned_out[...] = turned_ref[...]
    for write in writes:
        write.wait()


def per_device(hidden, head_weight, targets, response_mask, pair_ids, ref_logprobs):
    vmem = pl.BlockSpec(memory_space=pltpu.VMEM)
    smem = pl.BlockSpec(memory_space=pltpu.SMEM)
    hbm = pl.BlockSpec(memory_space=pl.ANY)
    copies = 448
    logprobs, turned, grad_weight = pl.pallas_call(
        kernel,
        out_shape=(
            jax.ShapeDtypeStruct((1, SEQS), F32),
            jax.ShapeDtypeStruct((WIDE, ROWS), BF16),
            jax.ShapeDtypeStruct(head_weight.shape, BF16),
        ),
        in_specs=[smem, smem, vmem, hbm, vmem, vmem],
        out_specs=(vmem, vmem, hbm),
        scratch_shapes=[
            pltpu.VMEM((8, 4, 4, 2, BLOB, TILE, LANES), BF16),
            pltpu.VMEM((8, 4, 4, 2, BLOB, TILE, LANES), BF16),
            pltpu.VMEM((PAIRS * PADDED, COLS), BF16),
            pltpu.VMEM((TOK, COLS), F32),
            pltpu.VMEM((TOK, COLS), BF16),
            pltpu.VMEM((7, TILE, LANES), BF16),
            pltpu.VMEM((7, TILE, LANES), BF16),
            pltpu.VMEM((2, 8, LANES), F32),
            pltpu.VMEM((2, 8, 2, 8, LANES), F32),
            pltpu.VMEM((4, 2, 8, LANES), F32),
            pltpu.VMEM((BLOB, TILE, LANES), F32),
            pltpu.VMEM((8, 4, 4, BLOB, TILE, LANES), BF16),
            pltpu.VMEM((4, TILE, LANES), BF16),
            pltpu.SemaphoreType.DMA((copies,)),
            pltpu.SemaphoreType.DMA((copies,)),
            pltpu.SemaphoreType.DMA((PAIRS,)),
            *reduce_shapes(),
        ],
        compiler_params=pltpu.CompilerParams(
            collective_id=0, has_side_effects=True, vmem_limit_bytes=60 * 1024 * 1024
        ),
        cost_estimate=pl.CostEstimate(
            flops=6 * TOK * 5376 * COLS, bytes_accessed=12 * 1024 * 1024, transcendentals=2 * TOK * COLS
        ),
    )(
        pair_ids, ref_logprobs, hidden.T, head_weight,
        targets.reshape(TOK // LANES, LANES), response_mask.reshape(TOK // LANES, LANES),
    )
    logprobs, turned, grad_weight = pl.pallas_call(
        move,
        out_shape=(
            jax.ShapeDtypeStruct((1, SEQS), F32),
            jax.ShapeDtypeStruct((WIDE, ROWS), BF16),
            jax.ShapeDtypeStruct(head_weight.shape, BF16),
        ),
        in_specs=[vmem, vmem, vmem],
        out_specs=(vmem, vmem, hbm),
        scratch_shapes=[
            pltpu.SemaphoreType.DMA((PAIRS,)),
        ],
        compiler_params=pltpu.CompilerParams(vmem_limit_bytes=16 * 1024 * 1024),
    )(logprobs, turned, grad_weight)
    return (logprobs.reshape(SEQS), turned.T, grad_weight)


def solution(mesh):
    placed = (
        P("dp", ("section", "tensor")),
        P(None, ("section", "tensor", "dp")),
        P(),
        P(),
        P(),
        P(),
    )
    return jax.shard_map(
        per_device,
        mesh=mesh,
        in_specs=placed,
        out_specs=(P(), P("dp", ("section", "tensor")), P(None, ("section", "tensor", "dp"))),
        check_vma=False,
    )
```
